32 devices in a mesh: rows: 4 (over z), cols: 8 (over y, x, core).
Axes of the slice: x: 2, y: 2, z: 4, core: 2. Of those that a mesh axis runs over, the one named last changes fastest.
Arguments:
- whitened: float32 [3, 131072], P(None, ('rows', 'cols')), may hold values from -6 to 6
- cotangent: bfloat16 [64, 131072], P(None, ('rows', 'cols')), may hold values from -6 to 6
- lift_weight: float32 [64, 3], replicated, may hold values from -3.5 to 3.5
- conv_now: bfloat16 [3, 128, 64], replicated, may hold values from -0.5 to 0.5
- conv_past: bfloat16 [3, 128, 64], replicated, may hold values from -0.5 to 0.5
- mix_weight: bfloat16 [3, 64, 64], replicated, may hold values from -0.75 to 0.75
- dilations: int32 [3], replicated, may hold values from 64 to 256, as said below
- psd_bin: int32 [4096, 8, 4], P(None, 'cols', 'rows'), may hold values from 0 to 1023, as said below
- psd_weight: float32 [2, 1024], replicated, may hold values from 0.2 to 5
Outputs:
- data_grad: float32 [3, 131072], P(None, ('rows', 'cols'))
- grad_now: float32 [3, 128, 64], replicated
- grad_past: float32 [3, 128, 64], replicated
- grad_mix: float32 [3, 64, 64], replicated
- grad_lift: float32 [64, 3], replicated
The draws below stay inside these ranges and needn't reach their ends.
Inputs may be any that keep to these rules, and one draw needn't show every extreme that they name: `dilations`: multiples of 4; one layer has 64, one has 256. `psd_bin`: frequencies k and 131072 - k have the same bin.
All inputs are finite; a program needn't handle non-finite values.
Results may differ from the reference program's by a relative error of at most 0.0068.
Values may be sent and summed in bfloat16 or wider, within the bound.
A program may use at most 64 MiB of HBM per device.

```python
import math
import jax
import jax.numpy as jnp
from jax import lax

C = 64
LAYERS = 3
DMAX = 256
NBINS = 1024
SEG = 4096
ROW_BLOCKS = 4
COL_BLOCKS = 8
LEN = 131072


def draw_dilations(key, part):
    middle_key = jax.random.fold_in(key, 11)
    order_key = jax.random.fold_in(key, 23)
    middle = 4 * jax.random.randint(middle_key, (), DMAX // 16, DMAX // 4 + 1, dtype=jnp.int32)
    levels = jnp.stack([jnp.int32(DMAX // 4), middle, jnp.int32(DMAX)]).astype(jnp.int32)
    return jax.random.permutation(order_key, levels)


def draw_psd_bin(key, part):
    length_all = SEG * ROW_BLOCKS * COL_BLOCKS
    raw_bins = jax.random.randint(key, (length_all,), 0, NBINS, dtype=jnp.int32)
    raw_bins = raw_bins.at[1].set(NBINS - 1).at[2].set(0)
    position = jnp.arange(length_all, dtype=jnp.int32)
    mirror = jnp.minimum(position, (length_all - position) % length_all)
    return raw_bins[mirror].reshape(SEG, COL_BLOCKS, ROW_BLOCKS)


def steps_of(key, extent, cuts, low, top_value):
    def one(axis_at, parts):
        draws = jax.random.uniform(jax.random.fold_in(jax.random.fold_in(key, 6), axis_at), (parts,), jnp.float32, low / len(cuts), top_value / len(cuts))
        return jnp.repeat(jnp.exp(draws), extent[axis_at] // parts).reshape((-1,) + (1,) * (len(extent) - axis_at - 1))

    gain = one(*cuts[0])
    for cut in cuts[1:]:
        gain = gain * one(*cut)
    return gain


def scatter_about(key, dims, scale, limit, split=(), held_as=jnp.bfloat16):
    level = steps_of(key, dims, split, -0.22, 0.18) if split else 1.0
    values = jax.random.normal(key, dims, jnp.float32) * scale * level
    return jnp.minimum(jnp.maximum(values, -limit), limit).astype(held_as)


def setup_inputs(seed: int = 0) -> dict:
    seeds = jax.random.split(jax.random.key(seed), 10)
    whitened = scatter_about(seeds[0], (3, LEN), 1.0, 6.0, ((1, 32),), jnp.float32)
    cotangent = scatter_about(seeds[1], (C, LEN), 1.0, 6.0, ((1, 32),))
    lift_weight = scatter_about(seeds[2], (C, 3), 3 ** -0.5, 3.5, (), jnp.float32)
    conv_now = scatter_about(seeds[3], (LAYERS, 2 * C, C), (2 * C) ** -0.5, 0.5)
    conv_past = scatter_about(seeds[4], (LAYERS, 2 * C, C), (2 * C) ** -0.5, 0.5)
    mix_weight = scatter_about(seeds[5], (LAYERS, C, C), C ** -0.5, 0.75)
    dilations = draw_dilations(jax.random.fold_in(seeds[9], 71), 0)
    psd_bin = draw_psd_bin(jax.random.fold_in(seeds[9], 71), 0)
    psd_weight = jnp.clip(jnp.exp(jax.random.uniform(seeds[8], (2, NBINS), jnp.float32, math.log(0.2), math.log(5.0))), 0.2, 5.0)
    return dict(whitened=whitened, cotangent=cotangent, lift_weight=lift_weight, conv_now=conv_now, conv_past=conv_past, mix_weight=mix_weight, dilations=dilations, psd_bin=psd_bin, psd_weight=psd_weight)


def lifted(lift_weight, inputs):
    return lift_weight[:, 0:1] * inputs[0:1] + lift_weight[:, 1:2] * inputs[1:2] + lift_weight[:, 2:3] * inputs[2:3]

def delayed(field_b, delay):
    joined = jnp.concatenate([jnp.zeros((field_b.shape[0], DMAX), field_b.dtype), field_b], axis=1)
    return lax.dynamic_slice_in_dim(joined, (DMAX - delay).astype(jnp.int32), field_b.shape[1], 1)

def advanced(values, delay, head_rim):
    joined = jnp.concatenate([values, head_rim], axis=1)
    return lax.dynamic_slice_in_dim(joined, delay.astype(jnp.int32), values.shape[1], 1)

def block_grads(window, cot_block, heads, lift_weight, conv_now, conv_past, mix_weight, dilations):
    channel_count = mix_weight.shape[1]
    margin = 3 * DMAX
    field_now = lifted(lift_weight, window)
    saved = []
    for layer_id in range(LAYERS):
        field_b = field_now.astype(jnp.bfloat16)
        past_b = delayed(field_b, dilations[layer_id])
        pre_act = jnp.dot(conv_now[layer_id], field_b, preferred_element_type=jnp.float32) + jnp.dot(conv_past[layer_id], past_b, preferred_element_type=jnp.float32)
        tanh_part = jnp.tanh(pre_act[:channel_count])
        sigm_part = jax.nn.sigmoid(pre_act[channel_count:])
        gate_b = (tanh_part * sigm_part).astype(jnp.bfloat16)
        saved.append((field_b[:, margin:], past_b[:, margin:], tanh_part[:, margin:], sigm_part[:, margin:], gate_b[:, margin:]))
        field_now = field_now + jnp.dot(mix_weight[layer_id], gate_b, preferred_element_type=jnp.float32)
    grad_field = cot_block.astype(jnp.float32)
    grads_now = [None] * LAYERS
    grads_past = [None] * LAYERS
    grads_mix = [None] * LAYERS
    new_heads = [None] * LAYERS
    for layer_id in reversed(range(LAYERS)):
        field_b, past_b, tanh_part, sigm_part, gate_b = saved[layer_id]
        grad_field_b = grad_field.astype(jnp.bfloat16)
        grad_gate = jnp.dot(mix_weight[layer_id].T, grad_field_b, preferred_element_type=jnp.float32)
        grads_mix[layer_id] = jnp.dot(grad_field_b, gate_b.T, preferred_element_type=jnp.float32)
        grad_pre = jnp.concatenate([grad_gate * sigm_part * (1.0 - tanh_part * tanh_part), grad_gate * tanh_part * sigm_part * (1.0 - sigm_part)], axis=0).astype(jnp.bfloat16)
        grads_now[layer_id] = jnp.dot(grad_pre, field_b.T, preferred_element_type=jnp.float32)
        grads_past[layer_id] = jnp.dot(grad_pre, past_b.T, preferred_element_type=jnp.float32)
        ahead_term = jnp.dot(conv_past[layer_id].T, grad_pre, preferred_element_type=jnp.float32)
        new_heads[layer_id] = ahead_term[:, :DMAX]
        grad_field = grad_field + jnp.dot(conv_now[layer_id].T, grad_pre, preferred_element_type=jnp.float32) + advanced(ahead_term, dilations[layer_id], heads[layer_id])
    own_input = window[:, margin:]
    input_grad = jnp.dot(lift_weight.T, grad_field, precision=lax.Precision.HIGHEST)
    lift_part = jnp.dot(grad_field, own_input.T, precision=lax.Precision.HIGHEST)
    return (input_grad, jnp.stack(grads_now), jnp.stack(grads_past), jnp.stack(grads_mix), lift_part, tuple(new_heads))

def reference(whitened, cotangent, lift_weight, conv_now, conv_past, mix_weight, dilations, psd_bin, psd_weight):
    channel_count = mix_weight.shape[1]
    block_count = LEN // SEG
    margin = 3 * DMAX
    padded = jnp.concatenate([jnp.zeros((3, margin), whitened.dtype), whitened], axis=1)

    def step_block(carry, block_id):
        heads, sum_now, sum_past, sum_mix, sum_lift = carry
        start_at = (block_id * SEG).astype(jnp.int32)
        window = lax.dynamic_slice_in_dim(padded, start_at, margin + SEG, 1)
        cot_block = lax.dynamic_slice_in_dim(cotangent, start_at, SEG, 1)
        input_grad, part_now, part_past, part_mix, part_lift, new_heads = block_grads(window, cot_block, heads, lift_weight, conv_now, conv_past, mix_weight, dilations)
        return ((new_heads, sum_now + part_now, sum_past + part_past, sum_mix + part_mix, sum_lift + part_lift), input_grad)
    start_heads = tuple((jnp.zeros((channel_count, DMAX), jnp.float32) for layer_id in range(LAYERS)))
    start_carry = (start_heads, jnp.zeros((LAYERS, 2 * channel_count, channel_count), jnp.float32), jnp.zeros((LAYERS, 2 * channel_count, channel_count), jnp.float32), jnp.zeros((LAYERS, channel_count, channel_count), jnp.float32), jnp.zeros((channel_count, 3), jnp.float32))
    final_carry, pieces = lax.scan(step_block, start_carry, jnp.arange(block_count, dtype=jnp.int32), reverse=True)
    input_grad = jnp.transpose(pieces, (1, 0, 2)).reshape(3, LEN)
    scaling = 1.0 / jnp.sqrt(jnp.float32(LEN))
    bins_flat = psd_bin.reshape(-1)
    weights = psd_weight[:, bins_flat]
    factors = jnp.stack([weights[0], weights[0], weights[1]])
    spectrum = jnp.fft.fft(input_grad, axis=1)
    data_grad = jnp.real(jnp.fft.ifft(spectrum * factors, axis=1)).astype(jnp.float32)
    return (data_grad, final_carry[1] * scaling, final_carry[2] * scaling, final_carry[3] * scaling, final_carry[4] * scaling)
```

```python
import math

import jax
import jax.numpy as jnp
import numpy as np
from jax import lax
from jax.experimental import pallas as pl
from jax.experimental.pallas import tpu as pltpu
from jax.sharding import PartitionSpec as P

DMAX = 256
TILE = 128
MARGIN = 640
FRONT = 384
F32 = jnp.float32
BF16 = jnp.bfloat16


def halves(matrix):
    high = matrix.astype(np.float32).astype(jnp.bfloat16)
    low = (matrix - high.astype(np.float64)).astype(np.float32).astype(jnp.bfloat16)
    return np.stack([high, low])


def split(values):
    high = values.astype(BF16)
    return high, (values - high.astype(F32)).astype(BF16)


def dot_left(pair_ref, values):
    high, low = split(values)
    total = jnp.dot(pair_ref[0], high, preferred_element_type=F32)
    total += jnp.dot(pair_ref[0], low, preferred_element_type=F32)
    return total + jnp.dot(pair_ref[1], high, preferred_element_type=F32)


def dot_right(values, pair_ref):
    high, low = split(values)
    total = jnp.dot(high, pair_ref[0], preferred_element_type=F32)
    total += jnp.dot(low, pair_ref[0], preferred_element_type=F32)
    return total + jnp.dot(high, pair_ref[1], preferred_element_type=F32)


def chunks_of(first, last, size=1024):
    cuts = sorted({first, last} | {x for x in range(0, last, size) if first < x < last})
    return list(zip(cuts[:-1], cuts[1:]))


def layers_kernel(
    dil_ref, white_ref, left_ref, right_ref, cot_ref, cot_right_ref, lift_ref, now_ref, past_ref,
    mix_ref, bins_ref, psd_ref,
    dinput_ref, grads_ref, factor_ref,
    inputs, cot, field, seen, gates, dfield, ahead,
):
    segment = white_ref.shape[1]
    layer_count = mix_ref.shape[0]
    channels = mix_ref.shape[1]
    lane = lax.broadcasted_iota(jnp.int32, (channels, TILE), 1)

    def at(column):
        return MARGIN + column

    bins = bins_ref[...]
    table_rows = psd_ref.shape[0] // 2
    row_at = lax.broadcasted_iota(jnp.int32, bins.shape, 0)
    first_row = jnp.where(lax.rem(row_at, 4) < 2, 0, table_rows)
    entry_row = lax.shift_right_logical(bins, 7) + first_row
    entry_lane = jnp.bitwise_and(bins, TILE - 1)
    factor = jnp.zeros(bins.shape, F32)
    for row in range(2 * table_rows):
        table = jnp.broadcast_to(psd_ref[row : row + 1, :], (bins.shape[0], TILE))
        found = jnp.take_along_axis(table, entry_lane, axis=1)
        factor = jnp.where(entry_row == row, found, factor)
    factor_ref[...] = factor

    inputs[:, 0:MARGIN] = left_ref[...]
    inputs[:, MARGIN : MARGIN + segment] = white_ref[...]
    inputs[:, MARGIN + segment :] = right_ref[...]
    cot[:, 0:segment] = cot_ref[...]
    cot[:, segment:] = cot_right_ref[...]

    lift = lift_ref[...]
    field[0, :, 0:FRONT] = jnp.zeros((channels, FRONT), F32)
    field[1, :, 0:FRONT] = jnp.zeros((channels, FRONT), F32)
    for start, stop in chunks_of(-MARGIN, segment + MARGIN):
        x = inputs[:, at(start) : at(stop)]
        field[0, :, FRONT + at(start) : FRONT + at(stop)] = (
            lift[:, 0:1] * x[0:1] + lift[:, 1:2] * x[1:2] + lift[:, 2:3] * x[2:3]
        )

    for layer in range(layer_count):
        delay = dil_ref[layer]
        tiles_back = delay // TILE
        rest = delay - tiles_back * TILE
        weight = jnp.concatenate([now_ref[layer], past_ref[layer]], axis=1)
        mix = mix_ref[layer]
        source, target = layer % 2, (layer + 1) % 2
        first = -DMAX * (layer_count - 1 - layer)
        for start, stop in chunks_of(first, segment + MARGIN):
            size = stop - start
            place = FRONT + at(start)
            now = field[source, :, place : place + size]
            begin = pl.multiple_of(place - TILE - tiles_back * TILE, TILE)
            window = field[source, :, pl.ds(begin, size + TILE)]
            turned = [
                pltpu.roll(window[:, TILE * i : TILE * (i + 1)], rest, 1)
                for i in range(size // TILE + 1)
            ]
            past = jnp.concatenate(
                [
                    jnp.where(lane < rest, turned[i], turned[i + 1])
                    for i in range(size // TILE)
                ],
                axis=1,
            )
            both = jnp.concatenate([now, past], axis=0).astype(BF16)
            pre = jnp.dot(weight, both, preferred_element_type=F32)
            filt = jnp.tanh(pre[:channels])
            sig = 0.5 * jnp.tanh(0.5 * pre[channels:]) + 0.5
            gate = (filt * sig).astype(BF16)
            if layer + 1 < layer_count:
                field[target, :, place : place + size] = now + jnp.dot(
                    mix, gate, preferred_element_type=F32
                )
            if start >= 0:
                seen[layer, 0 : 2 * channels, start:stop] = both
                seen[layer, 2 * channels :, start:stop] = gate
                gates[layer, 0:channels, start:stop] = filt
                gates[layer, channels:, start:stop] = sig

    mixes = []
    ahead[...] = jnp.zeros(ahead.shape, F32)
    for layer in reversed(range(layer_count)):
        delay = dil_ref[layer]
        tiles_on = delay // TILE
        rest = delay - tiles_on * TILE
        back = jnp.where(rest == 0, 0, TILE - rest)
        weight_t = jnp.concatenate([now_ref[layer], past_ref[layer]], axis=1).T
        mix_t = mix_ref[layer].T
        reach = min(MARGIN, DMAX * (layer + 1))
        total = jnp.zeros((3 * channels, 3 * channels), F32)
        for start, stop in reversed(chunks_of(0, segment + reach)):
            size = stop - start
            if layer == layer_count - 1:
                grad_b = cot[:, start:stop]
                grad = grad_b.astype(F32)
            else:
                grad = dfield[:, start:stop]
                grad_b = grad.astype(BF16)
            filt = gates[layer, 0:channels, start:stop]
            sig = gates[layer, channels:, start:stop]
            dgate = jnp.dot(mix_t, grad_b, preferred_element_type=F32)
            dgate_sig = dgate * sig
            dpre = jnp.concatenate(
                [dgate_sig * (1.0 - filt * filt), dgate_sig * filt * (1.0 - sig)], axis=0
            ).astype(BF16)
            terms = jnp.dot(weight_t, dpre, preferred_element_type=F32)
            ahead[:, start:stop] = terms[channels:]
            begin = pl.multiple_of(start + tiles_on * TILE, TILE)
            window = ahead[:, pl.ds(begin, size + TILE)]
            turned = [
                pltpu.roll(window[:, TILE * i : TILE * (i + 1)], back, 1)
                for i in range(size // TILE + 1)
            ]
            moved = jnp.concatenate(
                [
                    jnp.where(lane < TILE - rest, turned[i], turned[i + 1])
                    for i in range(size // TILE)
                ],
                axis=1,
            )
            dfield[:, start:stop] = grad + terms[:channels] + moved
            if start < segment:
                left = jnp.concatenate([dpre, grad_b], axis=0)
                total += lax.dot_general(
                    left, seen[layer, :, start:stop], (((1,), (1,)), ((), ())),
                    preferred_element_type=F32,
                )
        grads_ref[2 * channels * layer : 2 * channels * (layer + 1), :] = total[
            : 2 * channels, : 2 * channels
        ].astype(BF16)
        mixes.append(total[2 * channels :, 2 * channels :])

    lift_total = jnp.zeros((channels, 3), F32)
    lift_t = lift.T
    for start, stop in chunks_of(0, segment):
        grad = dfield[:, start:stop]
        x = inputs[:, at(start) : at(stop)]
        part = jnp.dot(lift_t, grad, preferred_element_type=F32, precision=lax.Precision.HIGHEST)
        part = jnp.concatenate([part, jnp.zeros((1, stop - start), F32)], axis=0)
        if dinput_ref.ndim == 3:
            for i in range((stop - start) // TILE):
                dinput_ref[start // TILE + i] = part[:, TILE * i : TILE * (i + 1)]
        else:
            dinput_ref[:, start:stop] = part
        lift_total += lax.dot_general(
            grad, x, (((1,), (1,)), ((), ())), preferred_element_type=F32,
            precision=lax.Precision.HIGHEST,
        )
    last = 2 * channels * layer_count
    grads_ref[last : last + channels, :] = jnp.concatenate([mixes[2], mixes[1]], axis=1).astype(BF16)
    grads_ref[last + channels :, :] = jnp.concatenate(
        [mixes[0], lift_total, jnp.zeros((channels, channels - 3), F32)], axis=1
    ).astype(BF16)


def filter_kernel(
    rows_count, cols_count,
    x_ref, grads_ref, factor_ref, turn_a_ref, turn_b_ref, spread_ref, local_ref, fast_ref,
    fast_back_ref, local_back_ref, gather_ref, twiddle_ref,
    out_ref, sums_ref,
    got_x, spectra, got_spectra, parts, got_parts, result, got_result, got_grads, own_sum, all_sums,
    send_sems, recv_sems,
):
    groups = rows_count * cols_count
    small = x_ref.shape[2]
    me = lax.axis_index("rows") * cols_count + lax.axis_index("cols")

    def peer_of(step):
        peer = lax.rem(me + step, groups)
        return peer, (peer // cols_count, lax.rem(peer, cols_count))

    barrier = pltpu.get_barrier_semaphore()

    def greet(step, carry):
        _, device = peer_of(step)
        pl.semaphore_signal(barrier, inc=1, device_id=device, device_id_type=pl.DeviceIdType.MESH)
        return carry

    lax.fori_loop(1, groups, greet, 0)
    pl.semaphore_wait(barrier, groups - 1)

    def exchange(slot, source, target, whole=False):
        def send(step, carry):
            peer, device = peer_of(step)
            pltpu.make_async_remote_copy(
                src_ref=source if whole else source.at[peer],
                dst_ref=target.at[me],
                send_sem=send_sems.at[slot],
                recv_sem=recv_sems.at[slot],
                device_id=device,
                device_id_type=pl.DeviceIdType.MESH,
            ).start()
            return carry

        lax.fori_loop(1, groups, send, 0)
        target[me] = source[...] if whole else source[me]

    def wait_for(sems, slot, target):
        some = target.at[pl.ds(0, groups - 1)]
        pltpu.make_async_copy(some, some, sems.at[slot]).wait()

    flat = (4 * groups, small)
    cube = (groups, 4, small)
    exchange(0, x_ref, got_x)
    exchange(1, grads_ref, got_grads)

    wait_for(recv_sems, 0, got_x)
    both = dot_left(spread_ref, got_x[...].reshape(flat))
    spectra[...] = (
        both[: 4 * groups] * turn_a_ref[0] + both[4 * groups :] * turn_a_ref[1]
    ).reshape(cube)
    exchange(2, spectra, got_spectra)

    wait_for(recv_sems, 1, got_grads)
    total = got_grads[0].astype(F32)
    for i in range(1, groups):
        total += got_grads[i].astype(F32)
    own_sum[...] = total.astype(BF16)
    exchange(3, own_sum, all_sums, whole=True)

    wait_for(recv_sems, 2, got_spectra)
    both = dot_left(local_ref, got_spectra[...].reshape(flat))
    here, turned = both[: 4 * groups], both[4 * groups :]
    cosine, sine = twiddle_ref[0], twiddle_ref[1]
    pair = jnp.concatenate([here * cosine - turned * sine, turned * cosine + here * sine], axis=1)
    pair = dot_right(pair, fast_ref)
    factor = factor_ref[...]
    pair = jnp.concatenate([pair[:, :small] * factor, pair[:, small:] * factor], axis=1)
    pair = dot_right(pair, fast_back_ref)
    here, turned = pair[:, :small], pair[:, small:]
    pair = jnp.concatenate([here * cosine + turned * sine, turned * cosine - here * sine], axis=1)
    pair = dot_left(local_back_ref, pair)
    parts[...] = (pair[:, :small] * turn_b_ref[0] + pair[:, small:] * turn_b_ref[1]).reshape(cube)
    exchange(4, parts, got_parts)

    wait_for(recv_sems, 4, got_parts)
    result[...] = dot_left(gather_ref, got_parts[...].reshape(flat)).reshape(cube)
    exchange(5, result, got_result)

    wait_for(recv_sems, 3, all_sums)
    sums_ref[...] = all_sums[...]
    wait_for(recv_sems, 5, got_result)
    if out_ref.ndim == 2:
        for i in range(groups):
            out_ref[:, small * i : small * (i + 1)] = got_result[i][:3]
    else:
        out_ref[...] = got_result[...]
    for slot, target in enumerate(
        (got_x, got_grads, got_spectra, all_sums, got_parts, got_result)
    ):
        wait_for(send_sems, slot, target)


def constants(rows_count, cols_count, small):
    groups = rows_count * cols_count
    segment = groups * small
    ids = np.arange(groups)
    residues = ids // cols_count + rows_count * (ids % cols_count)
    unit = np.eye(4)
    swap = np.kron(np.eye(2), np.array([[0.0, -1.0], [1.0, 0.0]]))
    take = np.diag([1.0, 1.0, 1.0, 0.0])

    def blocks(left, right, sign, inner):
        angle = sign * 2.0 * np.pi / groups * (np.outer(left, right) % groups)
        return np.kron(np.cos(angle), unit @ inner) + np.kron(np.sin(angle), swap @ inner)

    turn_all = np.kron(np.eye(groups), swap)
    spread = blocks(residues, ids, -1.0, take)
    local = blocks(ids, ids, -1.0, unit)
    local_back = blocks(ids, ids, 1.0, unit)
    gather = np.kron(np.eye(groups), take) @ blocks(ids, residues, 1.0, unit)
    gather = gather / float(segment * groups)
    lanes = np.arange(small)
    angle = 2.0 * np.pi / small * (np.outer(lanes, lanes) % small)
    cosine, sine = np.cos(angle), np.sin(angle)
    fast = np.block([[cosine, sine], [-sine, cosine]])
    fast_back = np.block([[cosine, -sine], [sine, cosine]])
    angle = 2.0 * np.pi / segment * (np.outer(ids, lanes) % segment)
    angle = np.repeat(angle, 4, axis=0)
    twiddle = np.stack([np.cos(angle), np.sin(angle)]).astype(np.float32)
    return (
        residues,
        halves(np.concatenate([spread, turn_all @ spread])),
        halves(np.concatenate([local, turn_all @ local])),
        halves(fast),
        halves(fast_back),
        halves(local_back),
        halves(gather),
        twiddle,
    )


def turns(angle_steps, length, sign):
    angle = sign * 2.0 * math.pi / length * (angle_steps % length).astype(F32)
    angle = jnp.repeat(angle, 4, axis=0)
    return jnp.stack([jnp.cos(angle), jnp.sin(angle)])


def vmem():
    return pl.BlockSpec(memory_space=pltpu.VMEM)


def solution(mesh):
    rows_count, cols_count = mesh.shape["rows"], mesh.shape["cols"]
    groups = rows_count * cols_count

    def local(whitened, cotangent, lift, now, past, mix, dilations, psd_bin, psd_weight):
        segment = whitened.shape[1]
        layer_count, channels = mix.shape[:2]
        small = segment // groups
        length = segment * groups
        me = lax.axis_index("rows") * cols_count + lax.axis_index("cols")
        residue = lax.axis_index("rows") + rows_count * lax.axis_index("cols")
        onward = [(i, i + 1) for i in range(groups - 1)]
        backward = [(i + 1, i) for i in range(groups - 1)]
        both_axes = ("rows", "cols")
        cot_right = lax.ppermute(cotangent[:, :MARGIN], both_axes, backward)
        left = lax.ppermute(whitened[:, segment - MARGIN :], both_axes, onward)
        right = lax.ppermute(whitened[:, :MARGIN], both_axes, backward)

        residues, spread, local_m, fast, fast_back, local_back, gather, twiddle = constants(
            rows_count, cols_count, small
        )
        samples = jnp.arange(small, dtype=jnp.int32)
        group_ids = jnp.arange(groups, dtype=jnp.int32)
        turn_a = turns(
            jnp.asarray(residues, jnp.int32)[:, None] * (me * small + samples)[None, :], length, -1.0
        )
        turn_b = turns(residue * (group_ids[:, None] * small + samples[None, :]), length, 1.0)

        wide = small == TILE
        bins = jnp.repeat(psd_bin.reshape(small, groups).T, 4, axis=0).reshape(-1, TILE)
        if not wide:
            bins = jnp.tile(psd_bin.reshape(small, groups).T.reshape(-1, 1, TILE), (1, 4, 1))
            bins = bins.reshape(-1, TILE)
        dinput_shape = (groups, 4, small) if wide else (4, segment)
        grad_rows = 2 * channels * (layer_count + 1)
        reach = segment + MARGIN
        dinput, grads, factor = pl.pallas_call(
            layers_kernel,
            out_shape=(
                jax.ShapeDtypeStruct(dinput_shape, F32),
                jax.ShapeDtypeStruct((grad_rows, 2 * channels), BF16),
                jax.ShapeDtypeStruct(bins.shape, F32),
            ),
            in_specs=[pl.BlockSpec(memory_space=pltpu.SMEM)] + [vmem()] * 11,
            out_specs=(vmem(),) * 3,
            scratch_shapes=[
                pltpu.VMEM((3, reach + MARGIN), F32),
                pltpu.VMEM((channels, reach), BF16),
                pltpu.VMEM((2, channels, FRONT + MARGIN + reach), F32),
                pltpu.VMEM((layer_count, 3 * channels, reach), BF16),
                pltpu.VMEM((layer_count, 2 * channels, reach), F32),
                pltpu.VMEM((channels, reach), F32),
                pltpu.VMEM((channels, reach + 3 * TILE), F32),
            ],
            compiler_params=pltpu.CompilerParams(vmem_limit_bytes=48 * 2**20),
            name="layers",
        )(
            dilations, whitened, left, right, cotangent, cot_right, lift, now, past, mix, bins,
            psd_weight.reshape(-1, TILE),
        )
        if not wide:
            dinput = dinput.reshape(4, groups, small).transpose(1, 0, 2)
            factor = factor.reshape(-1, 4, TILE).transpose(1, 0, 2).reshape(4, groups, small)
            factor = factor.transpose(1, 0, 2).reshape(4 * groups, small)
        cube = (groups, 4, small)
        share = (groups, grad_rows // groups, 2 * channels)
        out, sums = pl.pallas_call(
            lambda *refs: filter_kernel(rows_count, cols_count, *refs),
            out_shape=(
                jax.ShapeDtypeStruct((3, segment) if wide else cube, F32),
                jax.ShapeDtypeStruct(share, BF16),
            ),
            in_specs=[vmem()] * 12,
            out_specs=(vmem(),) * 2,
            scratch_shapes=[pltpu.VMEM(cube, F32)] * 7
            + [
                pltpu.VMEM(share, BF16),
                pltpu.VMEM(share[1:], BF16),
                pltpu.VMEM(share, BF16),
                pltpu.SemaphoreType.DMA((6,)),
                pltpu.SemaphoreType.DMA((6,)),
            ],
            compiler_params=pltpu.CompilerParams(
                collective_id=0, has_side_effects=True, vmem_limit_bytes=56 * 2**20
            ),
            name="whiten",
        )(
            dinput, grads.reshape(share), factor, turn_a, turn_b, spread, local_m, fast, fast_back,
            local_back, gather, twiddle,
        )
        if not wide:
            out = out.transpose(1, 0, 2).reshape(4, segment)[:3]
        scaling = 1.0 / math.sqrt(float(length))
        sums = sums.reshape(grad_rows, 2 * channels).astype(F32) * scaling
        last = 2 * channels * layer_count
        taps = sums[:last].reshape(layer_count, 2 * channels, 2 * channels)
        pair = sums[last : last + channels]
        rest = sums[last + channels :]
        mixes = jnp.stack([pair[:, :channels], pair[:, channels:], rest[:, :channels]])
        return (
            out,
            taps[:, :, :channels],
            taps[:, :, channels:],
            mixes,
            rest[:, channels : channels + 3],
        )

    in_specs = (
        P(None, ("rows", "cols")),
        P(None, ("rows", "cols")),
        P(),
        P(),
        P(),
        P(),
        P(),
        P(None, "cols", "rows"),
        P(),
    )
    out_specs = (P(None, ("rows", "cols")), P(), P(), P(), P())
    return jax.shard_map(local, mesh=mesh, in_specs=in_specs, out_specs=out_specs, check_vma=False)
```

```python
import math

import jax
import jax.numpy as jnp
import numpy as np
from jax import lax
from jax.experimental import pallas as pl
from jax.experimental.pallas import tpu as pltpu
from jax.sharding import PartitionSpec as P

DMAX = 256
TILE = 128
WIDE = 256
MARGIN = 640
FRONT = 384
F32 = jnp.float32
BF16 = jnp.bfloat16


def halves(matrix):
    high = matrix.astype(np.float32).astype(jnp.bfloat16)
    low = (matrix - high.astype(np.float64)).astype(np.float32).astype(jnp.bfloat16)
    return np.stack([high, low])


def split(values):
    high = values.astype(BF16)
    return high, (values - high.astype(F32)).astype(BF16)


def dot_left(pair_ref, values):
    high, low = split(values)
    total = jnp.dot(pair_ref[0], high, preferred_element_type=F32)
    total += jnp.dot(pair_ref[0], low, preferred_element_type=F32)
    return total + jnp.dot(pair_ref[1], high, preferred_element_type=F32)


def dot_right(values, pair_ref):
    high, low = split(values)
    total = jnp.dot(high, pair_ref[0], preferred_element_type=F32)
    total += jnp.dot(low, pair_ref[0], preferred_element_type=F32)
    return total + jnp.dot(high, pair_ref[1], preferred_element_type=F32)


def chunks_of(first, last, size=1024):
    cuts = sorted({first, last} | {x for x in range(0, last, size) if first < x < last})
    return list(zip(cuts[:-1], cuts[1:]))


def factors_kernel(bins_ref, psd_ref, factor_ref):
    bins = bins_ref[...]
    table_rows = psd_ref.shape[0] // 2
    row_at = lax.broadcasted_iota(jnp.int32, bins.shape, 0)
    first_row = jnp.where(lax.rem(row_at, 4) < 2, 0, table_rows)
    entry_row = lax.shift_right_logical(bins, 7) + first_row
    entry_lane = jnp.bitwise_and(bins, TILE - 1)
    factor = jnp.zeros(bins.shape, F32)
    for row in range(2 * table_rows):
        table = jnp.broadcast_to(psd_ref[row : row + 1, :], (bins.shape[0], TILE))
        found = jnp.take_along_axis(table, entry_lane, axis=1)
        factor = jnp.where(entry_row == row, found, factor)
    factor_ref[...] = factor


def layers(
    before_halos, halos,
    dil_ref, white_ref, cot_ref, lift_ref, now_ref, past_ref, mix_ref,
    dinput_ref, grads_ref, inputs, cot, field, seen, gates, dfield, ahead,
):
    segment = white_ref.shape[1]
    layer_count = mix_ref.shape[0]
    channels = mix_ref.shape[1]
    offset = lax.broadcasted_iota(jnp.int32, (DMAX + WIDE, WIDE), 0)
    offset -= lax.broadcasted_iota(jnp.int32, (DMAX + WIDE, WIDE), 1)

    def picks(distance):
        return jnp.where(offset == distance, 1.0, 0.0).astype(BF16)

    def moved(window, matrix):
        size = window.shape[1] - DMAX
        rows = window.shape[0]
        full = size // WIDE * WIDE
        pieces = []
        if full:
            stacked = jnp.concatenate(
                [window[:, i : i + DMAX + WIDE] for i in range(0, full, WIDE)], axis=0
            )
            found = jnp.dot(stacked, matrix, preferred_element_type=F32).astype(BF16)
            pieces = [found[rows * i : rows * (i + 1)] for i in range(full // WIDE)]
        if full < size:
            part = matrix[: DMAX + size - full, : size - full]
            found = jnp.dot(window[:, full:], part, preferred_element_type=F32)
            pieces.append(found.astype(BF16))
        return jnp.concatenate(pieces, axis=1)

    def at(column):
        return MARGIN + column

    inputs[:, MARGIN : MARGIN + segment] = white_ref[...]
    cot[:, 0:segment] = cot_ref[...]
    lift_t = lift_ref[...]
    lift = lift_t.T
    field[0, :, 0:FRONT] = jnp.zeros((channels, FRONT), F32)
    field[1, :, 0:FRONT] = jnp.zeros((channels, FRONT), F32)
    def lifted(start, stop):
        x = inputs[:, at(start) : at(stop)]
        field[0, :, FRONT + at(start) : FRONT + at(stop)] = (
            lift[:, 0:1] * x[0:1] + lift[:, 1:2] * x[1:2] + lift[:, 2:3] * x[2:3]
        )

    def in_order(layer, first):
        chunks = chunks_of(first, segment + MARGIN)
        if layer > 0:
            yield from chunks
            return
        inner = [c for c in chunks if DMAX <= c[0] and c[1] <= segment]
        yield from inner
        left, right, cot_right = halos()
        inputs[:, 0:MARGIN] = left
        inputs[:, MARGIN + segment :] = right
        cot[:, segment:] = cot_right
        lifted(-MARGIN, 0)
        lifted(segment, segment + MARGIN)
        yield from [c for c in chunks if c not in inner]

    for start, stop in chunks_of(0, segment):
        lifted(start, stop)
    before_halos()

    for layer in range(layer_count):
        delays = dil_ref[layer : layer + 1, :]
        matrix = picks(DMAX - delays)
        weight = jnp.concatenate([now_ref[layer], past_ref[layer]], axis=0).T
        mix = mix_ref[layer]
        source, target = layer % 2, (layer + 1) % 2
        first = -DMAX * (layer_count - 1 - layer)
        for start, stop in in_order(layer, first):
            size = stop - start
            place = FRONT + at(start)
            now = field[source, :, place : place + size]
            past = moved(field[source, :, place - DMAX : place + size].astype(BF16), matrix)
            both = jnp.concatenate([now.astype(BF16), past], axis=0)
            pre = jnp.dot(weight, both, preferred_element_type=F32)
            filt = jnp.tanh(pre[:channels])
            sig = 0.5 * jnp.tanh(0.5 * pre[channels:]) + 0.5
            gate = (filt * sig).astype(BF16)
            if layer + 1 < layer_count:
                field[target, :, place : place + size] = now + jnp.dot(
                    mix, gate, preferred_element_type=F32
                )
            if start >= 0:
                seen[layer, 0 : 2 * channels, start:stop] = both
                seen[layer, 2 * channels :, start:stop] = gate
                gates[layer, 0:channels, start:stop] = filt
                gates[layer, channels:, start:stop] = sig

    taps, mixes = [], []
    ahead[...] = jnp.zeros(ahead.shape, BF16)
    for layer in reversed(range(layer_count)):
        delays = dil_ref[layer : layer + 1, :]
        matrix = picks(delays)
        weight_t = jnp.concatenate([now_ref[layer], past_ref[layer]], axis=1)
        mix_t = mix_ref[layer].T
        reach = min(MARGIN, DMAX * (layer + 1))
        total = jnp.zeros((3 * channels, 3 * channels), F32)
        for start, stop in reversed(chunks_of(0, segment + reach)):
            size = stop - start
            if layer == layer_count - 1:
                grad_b = cot[:, start:stop]
                grad = grad_b.astype(F32)
            else:
                grad = dfield[:, start:stop]
                grad_b = grad.astype(BF16)
            filt = gates[layer, 0:channels, start:stop]
            sig = gates[layer, channels:, start:stop]
            dgate = jnp.dot(mix_t, grad_b, preferred_element_type=F32)
            dgate_sig = dgate * sig
            dpre = jnp.concatenate(
                [dgate_sig * (1.0 - filt * filt), dgate_sig * filt * (1.0 - sig)], axis=0
            ).astype(BF16)
            ahead[:, start:stop] = dpre
            later = moved(ahead[:, start : stop + DMAX], matrix)
            dfield[:, start:stop] = grad + jnp.dot(
                weight_t, jnp.concatenate([dpre, later], axis=0), preferred_element_type=F32
            )
            if start < segment:
                left = jnp.concatenate([dpre, grad_b], axis=0)
                total += lax.dot_general(
                    seen[layer, :, start:stop], left, (((1,), (1,)), ((), ())),
                    preferred_element_type=F32,
                )
        taps.insert(0, total[: 2 * channels, : 2 * channels])
        mixes.insert(0, total[2 * channels :, 2 * channels :].T)

    lift_total = jnp.zeros((3, channels), F32)
    for start, stop in chunks_of(0, segment):
        grad = dfield[:, start:stop]
        x = inputs[:, at(start) : at(stop)]
        part = jnp.dot(lift_t, grad, preferred_element_type=F32, precision=lax.Precision.HIGHEST)
        part = jnp.concatenate([part, jnp.zeros((1, stop - start), F32)], axis=0)
        small = dinput_ref.shape[2]
        for i in range((stop - start) // small):
            dinput_ref[start // small + i] = part[:, small * i : small * (i + 1)]
        lift_total += lax.dot_general(
            x, grad, (((1,), (1,)), ((), ())), preferred_element_type=F32,
            precision=lax.Precision.HIGHEST,
        )
    lift_block = jnp.concatenate([lift_total, jnp.zeros((channels - 3, channels), F32)], axis=0)
    taps.append(
        jnp.concatenate(
            [
                jnp.concatenate([mixes[0], mixes[1]], axis=1),
                jnp.concatenate([mixes[2], lift_block], axis=1),
            ],
            axis=0,
        )
    )
    rows = jnp.concatenate(taps, axis=0)
    grads_ref[...] = rows.reshape(grads_ref.shape).astype(BF16)


def whole_kernel(
    rows_count, cols_count,
    dil_ref, white_ref, cot_ref, lift_ref, now_ref, past_ref, mix_ref, factor_ref,
    cos_a_ref, sin_a_ref, cos_b_ref, sin_b_ref, spread_ref, local_ref, fast_ref,
    fast_back_ref, local_back_ref, gather_ref, twiddle_ref,
    out_ref, sums_ref,
    inputs, cot, field, seen, gates, dfield, ahead, left_halo, right_halo, cot_halo, dinput, grads,
    got_x, spectra, got_spectra, parts, got_parts, result, got_result,
    got_cols, part_sums, got_rows, own_sum, sums_rows, sums_all,
    send_sems, recv_sems,
):
    groups = rows_count * cols_count
    segment = white_ref.shape[1]
    small = segment // groups
    my_row, my_col = lax.axis_index("rows"), lax.axis_index("cols")
    me = my_row * cols_count + my_col
    cols = [my_col] + [lax.rem(my_col + j, cols_count) for j in range(1, cols_count)]
    rows = [my_row] + [lax.rem(my_row + i, rows_count) for i in range(1, rows_count)]

    def for_others(body):
        for col in cols[1:]:
            body(my_row, col)

        def one_row(step, carry):
            row = lax.rem(my_row + step, rows_count)
            for col in cols:
                body(row, col)
            return carry

        lax.fori_loop(1, rows_count, one_row, 0)

    def send(slot, source, target, row, col):
        pltpu.make_async_remote_copy(
            src_ref=source,
            dst_ref=target,
            send_sem=send_sems.at[slot],
            recv_sem=recv_sems.at[slot],
            device_id=(row, col),
            device_id_type=pl.DeviceIdType.MESH,
        ).start()

    def wait_for(sems, slot, landed):
        pltpu.make_async_copy(landed, landed, sems.at[slot]).wait()

    def exchange(slot, source, target):
        def one(row, col):
            send(slot, source.at[row * cols_count + col], target.at[me], row, col)

        for_others(one)
        target[me] = source[me]

    barrier = pltpu.get_barrier_semaphore()

    def greet(row, col):
        pl.semaphore_signal(
            barrier, inc=1, device_id=(row, col), device_id_type=pl.DeviceIdType.MESH
        )

    for_others(greet)

    after = lax.rem(me + 1, groups)
    ahead_of = lax.rem(me + groups - 1, groups)
    halo_slots = ((6, left_halo), (7, right_halo), (8, cot_halo))

    def before_halos():
        pl.semaphore_wait(barrier, groups - 1)
        row, col = after // cols_count, lax.rem(after, cols_count)
        send(6, white_ref.at[:, pl.ds(segment - MARGIN, MARGIN)], left_halo, row, col)
        row, col = ahead_of // cols_count, lax.rem(ahead_of, cols_count)
        send(7, white_ref.at[:, pl.ds(0, MARGIN)], right_halo, row, col)
        send(8, cot_ref.at[:, pl.ds(0, MARGIN)], cot_halo, row, col)

    def halos():
        for slot, landed in halo_slots:
            wait_for(recv_sems, slot, landed)
        left = jnp.where(me == 0, 0.0, left_halo[...])
        right = jnp.where(me == groups - 1, 0.0, right_halo[...])
        cot_right = jnp.where(me == groups - 1, 0.0, cot_halo[...].astype(F32)).astype(BF16)
        return left, right, cot_right

    layers(
        before_halos, halos,
        dil_ref, white_ref, cot_ref, lift_ref, now_ref, past_ref, mix_ref,
        dinput, grads, inputs, cot, field, seen, gates, dfield, ahead,
    )

    flat = (4 * groups, small)
    cube = (groups, 4, small)

    def turned_by(values, cos_ref, sin_ref):
        here, turned = values
        cosine = jnp.broadcast_to(cos_ref[...][:, None, :], cube).reshape(flat)
        sine = jnp.broadcast_to(sin_ref[...][:, None, :], cube).reshape(flat)
        return (here * cosine + turned * sine).reshape(cube)

    exchange(0, dinput, got_x)
    for col in cols[1:]:
        send(1, grads.at[:, col], got_cols.at[my_col], my_row, col)
    got_cols[my_col] = grads[:, my_col]

    wait_for(recv_sems, 0, got_x.at[pl.ds(0, groups - 1)])
    both = dot_left(spread_ref, got_x[...].reshape(flat))
    spectra[...] = turned_by((both[: 4 * groups], both[4 * groups :]), cos_a_ref, sin_a_ref)
    exchange(2, spectra, got_spectra)

    wait_for(recv_sems, 1, got_cols.at[pl.ds(0, cols_count - 1)])
    total = got_cols[0].astype(F32)
    for i in range(1, cols_count):
        total += got_cols[i].astype(F32)
    part_sums[...] = total
    for row in rows[1:]:
        send(3, part_sums.at[row], got_rows.at[my_row], row, my_col)
    got_rows[my_row] = part_sums[my_row]

    wait_for(recv_sems, 2, got_spectra.at[pl.ds(0, groups - 1)])
    both = dot_left(local_ref, got_spectra[...].reshape(flat))
    here, turned = both[: 4 * groups], both[4 * groups :]
    cosine, sine = twiddle_ref[0], twiddle_ref[1]
    pair = jnp.concatenate([here * cosine - turned * sine, turned * cosine + here * sine], axis=1)
    pair = dot_right(pair, fast_ref)
    factor = factor_ref[...]
    pair = jnp.concatenate([pair[:, :small] * factor, pair[:, small:] * factor], axis=1)
    pair = dot_right(pair, fast_back_ref)
    here, turned = pair[:, :small], pair[:, small:]
    pair = jnp.concatenate([here * cosine + turned * sine, turned * cosine - here * sine], axis=1)
    pair = dot_left(local_back_ref, pair)
    parts[...] = turned_by((pair[:, :small], pair[:, small:]), cos_b_ref, sin_b_ref)
    exchange(4, parts, got_parts)

    wait_for(recv_sems, 3, got_rows.at[pl.ds(0, rows_count - 1)])
    total = got_rows[0]
    for i in range(1, rows_count):
        total += got_rows[i]
    own_sum[...] = total.astype(BF16)
    for row in rows[1:]:
        send(9, own_sum, sums_rows.at[my_row], row, my_col)
    sums_rows[my_row] = own_sum[...]

    wait_for(recv_sems, 4, got_parts.at[pl.ds(0, groups - 1)])
    result[...] = dot_left(gather_ref, got_parts[...].reshape(flat)).reshape(cube)
    exchange(5, result, got_result)

    wait_for(recv_sems, 9, sums_rows.at[pl.ds(0, rows_count - 1)])
    for col in cols[1:]:
        send(10, sums_rows, sums_all.at[:, my_col], my_row, col)
    sums_all[:, my_col] = sums_rows[...]

    wait_for(recv_sems, 5, got_result.at[pl.ds(0, groups - 1)])
    out_ref[...] = got_result[...]
    wait_for(recv_sems, 10, sums_all.at[:, pl.ds(0, cols_count - 1)])
    sums_ref[...] = sums_all[...]

    for slot, sent in ((0, dinput), (2, spectra), (4, parts), (5, result)):
        wait_for(send_sems, slot, sent.at[pl.ds(0, groups - 1)])
    wait_for(send_sems, 1, got_cols.at[pl.ds(0, cols_count - 1)])
    wait_for(send_sems, 3, got_rows.at[pl.ds(0, rows_count - 1)])
    wait_for(send_sems, 9, sums_rows.at[pl.ds(0, rows_count - 1)])
    wait_for(send_sems, 10, sums_all.at[:, pl.ds(0, cols_count - 1)])
    for slot, landed in halo_slots:
        wait_for(send_sems, slot, landed)


def finish_kernel(scaling, out_ref, sums_ref, data_ref, now_ref, past_ref, mix_ref, lift_ref):
    layer_count, channels = mix_ref.shape[:2]
    if data_ref.ndim == 2:
        small = out_ref.shape[2]
        for i in range(out_ref.shape[0]):
            data_ref[:, small * i : small * (i + 1)] = out_ref[i][:3]
    else:
        data_ref[...] = out_ref[...]
    sums = sums_ref[...].astype(F32) * scaling
    for layer in range(layer_count):
        first = 2 * channels * layer
        now_ref[layer] = sums[first : first + channels]
        past_ref[layer] = sums[first + channels : first + 2 * channels]
    first = 2 * channels * layer_count
    mix_ref[0] = sums[first : first + channels, :channels]
    mix_ref[1] = sums[first : first + channels, channels:]
    mix_ref[2] = sums[first + channels :, :channels]
    lift_ref[...] = sums[first + channels : first + channels + 3, channels:]


def constants(rows_count, cols_count, small):
    groups = rows_count * cols_count
    segment = groups * small
    ids = np.arange(groups)
    residues = ids // cols_count + rows_count * (ids % cols_count)
    unit = np.eye(4)
    swap = np.kron(np.eye(2), np.array([[0.0, -1.0], [1.0, 0.0]]))
    take = np.diag([1.0, 1.0, 1.0, 0.0])

    def blocks(left, right, sign, inner):
        angle = sign * 2.0 * np.pi / groups * (np.outer(left, right) % groups)
        return np.kron(np.cos(angle), unit @ inner) + np.kron(np.sin(angle), swap @ inner)

    turn_all = np.kron(np.eye(groups), swap)
    spread = blocks(residues, ids, -1.0, take)
    local = blocks(ids, ids, -1.0, unit)
    local_back = blocks(ids, ids, 1.0, unit)
    gather = np.kron(np.eye(groups), take) @ blocks(ids, residues, 1.0, unit)
    gather = gather / float(segment * groups)
    lanes = np.arange(small)
    angle = 2.0 * np.pi / small * (np.outer(lanes, lanes) % small)
    cosine, sine = np.cos(angle), np.sin(angle)
    fast = np.block([[cosine, sine], [-sine, cosine]])
    fast_back = np.block([[cosine, -sine], [sine, cosine]])
    angle = 2.0 * np.pi / segment * (np.outer(ids, lanes) % segment)
    angle = np.repeat(angle, 4, axis=0)
    twiddle = np.stack([np.cos(angle), np.sin(angle)]).astype(np.float32)
    return (
        residues,
        halves(np.concatenate([spread, turn_all @ spread])),
        halves(np.concatenate([local, turn_all @ local])),
        halves(fast),
        halves(fast_back),
        halves(local_back),
        halves(gather),
        twiddle,
    )


def turns(angle_steps, length, sign):
    angle = sign * 2.0 * math.pi / length * (angle_steps % length).astype(F32)
    return jnp.cos(angle), jnp.sin(angle)


def vmem():
    return pl.BlockSpec(memory_space=pltpu.VMEM)


def solution(mesh):
    rows_count, cols_count = mesh.shape["rows"], mesh.shape["cols"]
    groups = rows_count * cols_count

    def local(whitened, cotangent, lift, now, past, mix, dilations, psd_bin, psd_weight):
        segment = whitened.shape[1]
        layer_count, channels = mix.shape[:2]
        small = segment // groups
        length = segment * groups
        me = lax.axis_index("rows") * cols_count + lax.axis_index("cols")
        residue = lax.axis_index("rows") + rows_count * lax.axis_index("cols")
        _, spread, local_m, fast, fast_back, local_back, gather, twiddle = constants(
            rows_count, cols_count, small
        )
        samples = lax.broadcasted_iota(jnp.int32, (groups, small), 1)
        ids = lax.broadcasted_iota(jnp.int32, (groups, small), 0)
        residues = ids // cols_count + rows_count * (ids % cols_count)
        cos_a, sin_a = turns(residues * (me * small + samples), length, -1.0)
        cos_b, sin_b = turns(residue * (ids * small + samples), length, 1.0)

        wide = small == TILE
        bins = psd_bin.reshape(small, groups).T
        bins = jnp.tile(bins.reshape(-1, 1, TILE), (1, 4, 1)).reshape(-1, TILE)
        factor = pl.pallas_call(
            factors_kernel,
            out_shape=jax.ShapeDtypeStruct(bins.shape, F32),
            in_specs=[vmem()] * 2,
            out_specs=vmem(),
            name="factors",
        )(bins, psd_weight.reshape(-1, TILE))
        if not wide:
            factor = factor.reshape(-1, 4, TILE).transpose(1, 0, 2).reshape(4, groups, small)
            factor = factor.transpose(1, 0, 2).reshape(4 * groups, small)

        grad_rows = 2 * channels * (layer_count + 1)
        reach = segment + MARGIN
        cube = (groups, 4, small)
        share = (grad_rows // groups, 2 * channels)
        shares = (rows_count, cols_count) + share
        out, sums = pl.pallas_call(
            lambda *refs: whole_kernel(rows_count, cols_count, *refs),
            out_shape=(
                jax.ShapeDtypeStruct(cube, F32),
                jax.ShapeDtypeStruct(shares, BF16),
            ),
            in_specs=[vmem()] * 19,
            out_specs=(vmem(),) * 2,
            scratch_shapes=[
                pltpu.VMEM((3, reach + MARGIN), F32),
                pltpu.VMEM((channels, reach), BF16),
                pltpu.VMEM((2, channels, FRONT + MARGIN + reach), F32),
                pltpu.VMEM((layer_count, 3 * channels, reach), BF16),
                pltpu.VMEM((layer_count, 2 * channels, reach), F32),
                pltpu.VMEM((channels, reach), F32),
                pltpu.VMEM((2 * channels, reach + DMAX), BF16),
                pltpu.VMEM((3, MARGIN), F32),
                pltpu.VMEM((3, MARGIN), F32),
                pltpu.VMEM((channels, MARGIN), BF16),
                pltpu.VMEM(cube, F32),
                pltpu.VMEM(shares, BF16),
            ]
            + [pltpu.VMEM(cube, F32)] * 7
            + [
                pltpu.VMEM((cols_count, rows_count) + share, BF16),
                pltpu.VMEM((rows_count,) + share, F32),
                pltpu.VMEM((rows_count,) + share, F32),
                pltpu.VMEM(share, BF16),
                pltpu.VMEM((rows_count,) + share, BF16),
                pltpu.VMEM(shares, BF16),
                pltpu.SemaphoreType.DMA((11,)),
                pltpu.SemaphoreType.DMA((11,)),
            ],
            compiler_params=pltpu.CompilerParams(
                collective_id=0, has_side_effects=True, vmem_limit_bytes=60 * 2**20
            ),
            name="whole",
        )(
            jnp.broadcast_to(dilations[:, None], (layer_count, WIDE)), whitened, cotangent, lift.T, now.transpose(0, 2, 1),
            past.transpose(0, 2, 1), mix, factor, cos_a, sin_a, cos_b, sin_b, spread, local_m,
            fast, fast_back, local_back, gather, twiddle,
        )
        scaling = 1.0 / math.sqrt(float(length))
        data, now_t, past_t, mixes, lift_t = pl.pallas_call(
            lambda *refs: finish_kernel(scaling, *refs),
            out_shape=(
                jax.ShapeDtypeStruct((3, segment) if wide else cube, F32),
                jax.ShapeDtypeStruct((layer_count, channels, 2 * channels), F32),
                jax.ShapeDtypeStruct((layer_count, channels, 2 * channels), F32),
                jax.ShapeDtypeStruct((layer_count, channels, channels), F32),
                jax.ShapeDtypeStruct((3, channels), F32),
            ),
            in_specs=[vmem()] * 2,
            out_specs=(vmem(),) * 5,
            name="finish",
        )(out, sums.reshape(grad_rows, 2 * channels))
        if not wide:
            data = data.transpose(1, 0, 2).reshape(4, segment)[:3]
        return data, now_t.transpose(0, 2, 1), past_t.transpose(0, 2, 1), mixes, lift_t.T

    in_specs = (
        P(None, ("rows", "cols")),
        P(None, ("rows", "cols")),
        P(),
        P(),
        P(),
        P(),
        P(),
        P(None, "cols", "rows"),
        P(),
    )
    out_specs = (P(None, ("rows", "cols")), P(), P(), P(), P())
    return jax.shard_map(local, mesh=mesh, in_specs=in_specs, out_specs=out_specs, check_vma=False)
```

```python
import math

import jax
import jax.numpy as jnp
import numpy as np
from jax import lax
from jax.experimental import pallas as pl
from jax.experimental.pallas import tpu as pltpu
from jax.sharding import PartitionSpec as P

DMAX = 256
TILE = 128
WIDE = 256
MARGIN = 640
FRONT = 384
F32 = jnp.float32
BF16 = jnp.bfloat16


def halves(matrix):
    high = matrix.astype(np.float32).astype(jnp.bfloat16)
    low = (matrix - high.astype(np.float64)).astype(np.float32).astype(jnp.bfloat16)
    return np.stack([high, low])


def split(values):
    high = values.astype(BF16)
    return high, (values - high.astype(F32)).astype(BF16)


def dot_left(pair_ref, values):
    high, low = split(values)
    total = jnp.dot(pair_ref[0], high, preferred_element_type=F32)
    total += jnp.dot(pair_ref[0], low, preferred_element_type=F32)
    return total + jnp.dot(pair_ref[1], high, preferred_element_type=F32)


def dot_right(values, pair_ref):
    high, low = split(values)
    total = jnp.dot(high, pair_ref[0], preferred_element_type=F32)
    total += jnp.dot(low, pair_ref[0], preferred_element_type=F32)
    return total + jnp.dot(high, pair_ref[1], preferred_element_type=F32)


def chunks_of(first, last, size=1024):
    cuts = sorted({first, last} | {x for x in range(0, last, size) if first < x < last})
    return list(zip(cuts[:-1], cuts[1:]))


def turns(angle_steps, length, sign):
    angle = sign * 2.0 * math.pi / length * lax.rem(angle_steps, length).astype(F32)
    return jnp.cos(angle), jnp.sin(angle)


def prepare_kernel(
    rows_count, cols_count, length,
    dil_ref, bins_ref, psd_ref,
    factor_ref, cos_a_ref, sin_a_ref, cos_b_ref, sin_b_ref, delays_ref,
):
    bins = bins_ref[...]
    entry_row = lax.shift_right_logical(bins, 7)
    entry_lane = jnp.bitwise_and(bins, TILE - 1)
    factors = []
    for kind in range(2):
        factor = jnp.zeros(bins.shape, F32)
        for row in range(psd_ref.shape[1] // TILE):
            table = psd_ref[kind : kind + 1, TILE * row : TILE * (row + 1)]
            table = jnp.broadcast_to(table, bins.shape)
            found = jnp.take_along_axis(table, entry_lane, axis=1)
            factor = jnp.where(entry_row == row, found, factor)
        factors.append(factor)
    signal = lax.broadcasted_iota(jnp.int32, (bins.shape[0], 4, TILE), 1)
    factor_ref[...] = jnp.where(
        signal < 2, factors[0][:, None, :], factors[1][:, None, :]
    ).reshape(factor_ref.shape)

    shape = cos_a_ref.shape
    groups, small = shape
    my_row, my_col = lax.axis_index("rows"), lax.axis_index("cols")
    me = my_row * cols_count + my_col
    residue = my_row + rows_count * my_col
    samples = lax.broadcasted_iota(jnp.int32, shape, 1)
    ids = lax.broadcasted_iota(jnp.int32, shape, 0)
    rows = sum((ids >= cols_count * i).astype(jnp.int32) for i in range(1, rows_count))
    residues = rows + rows_count * (ids - cols_count * rows)
    cos_a_ref[...], sin_a_ref[...] = turns(residues * (me * small + samples), length, -1.0)
    cos_b_ref[...], sin_b_ref[...] = turns(residue * (ids * small + samples), length, 1.0)
    for layer in range(dil_ref.shape[0]):
        delays_ref[layer : layer + 1, :] = jnp.full((1, WIDE), dil_ref[layer], jnp.int32)


def layers(
    before_halos, halos, leave,
    dil_ref, white_ref, cot_ref, lift_ref, now_ref, past_ref, mix_ref,
    dinput_ref, grads_ref, inputs, cot, field, seen, gates, dfield, ahead,
):
    segment = white_ref.shape[1]
    layer_count = mix_ref.shape[0]
    channels = mix_ref.shape[1]
    offset = lax.broadcasted_iota(jnp.int32, (DMAX + WIDE, WIDE), 0)
    offset -= lax.broadcasted_iota(jnp.int32, (DMAX + WIDE, WIDE), 1)

    def picks(distance):
        return jnp.where(offset == distance, 1.0, 0.0).astype(BF16)

    def moved(window, matrix):
        size = window.shape[1] - DMAX
        rows = window.shape[0]
        full = size // WIDE * WIDE
        pieces = []
        if full:
            stacked = jnp.concatenate(
                [window[:, i : i + DMAX + WIDE] for i in range(0, full, WIDE)], axis=0
            )
            found = jnp.dot(stacked, matrix, preferred_element_type=F32).astype(BF16)
            pieces = [found[rows * i : rows * (i + 1)] for i in range(full // WIDE)]
        if full < size:
            part = matrix[: DMAX + size - full, : size - full]
            found = jnp.dot(window[:, full:], part, preferred_element_type=F32)
            pieces.append(found.astype(BF16))
        return jnp.concatenate(pieces, axis=1)

    def at(column):
        return MARGIN + column

    inputs[:, MARGIN : MARGIN + segment] = white_ref[...]
    cot[:, 0:segment] = cot_ref[...]
    lift_t = lift_ref[...]
    lift = lift_t.T
    field[0, :, 0:FRONT] = jnp.zeros((channels, FRONT), F32)
    field[1, :, 0:FRONT] = jnp.zeros((channels, FRONT), F32)
    def lifted(start, stop):
        x = inputs[:, at(start) : at(stop)]
        field[0, :, FRONT + at(start) : FRONT + at(stop)] = (
            lift[:, 0:1] * x[0:1] + lift[:, 1:2] * x[1:2] + lift[:, 2:3] * x[2:3]
        )

    def in_order(layer, first):
        chunks = chunks_of(first, segment + MARGIN)
        if layer > 0:
            yield from chunks
            return
        inner = [c for c in chunks if DMAX <= c[0] and c[1] <= segment]
        yield from inner
        left, right, cot_right = halos()
        inputs[:, 0:MARGIN] = left
        inputs[:, MARGIN + segment :] = right
        cot[:, segment:] = cot_right
        lifted(-MARGIN, 0)
        lifted(segment, segment + MARGIN)
        yield from [c for c in chunks if c not in inner]

    for start, stop in chunks_of(0, segment):
        lifted(start, stop)
    before_halos()

    for layer in range(layer_count):
        delays = dil_ref[layer : layer + 1, :]
        matrix = picks(DMAX - delays)
        weight = jnp.concatenate([now_ref[layer], past_ref[layer]], axis=0).T
        mix = mix_ref[layer]
        source, target = layer % 2, (layer + 1) % 2
        first = -DMAX * (layer_count - 1 - layer)
        for start, stop in in_order(layer, first):
            size = stop - start
            place = FRONT + at(start)
            now = field[source, :, place : place + size]
            past = moved(field[source, :, place - DMAX : place + size].astype(BF16), matrix)
            both = jnp.concatenate([now.astype(BF16), past], axis=0)
            pre = jnp.dot(weight, both, preferred_element_type=F32)
            filt = jnp.tanh(pre[:channels])
            sig = 0.5 * jnp.tanh(0.5 * pre[channels:]) + 0.5
            gate = (filt * sig).astype(BF16)
            if layer + 1 < layer_count:
                field[target, :, place : place + size] = now + jnp.dot(
                    mix, gate, preferred_element_type=F32
                )
            if start >= 0:
                seen[layer, 0 : 2 * channels, start:stop] = both
                seen[layer, 2 * channels :, start:stop] = gate
                gates[layer, 0:channels, start:stop] = filt
                gates[layer, channels:, start:stop] = sig

    small = dinput_ref.shape[2]
    for layer in reversed(range(layer_count)):
        delays = dil_ref[layer : layer + 1, :]
        matrix = picks(delays)
        weight_t = jnp.concatenate([now_ref[layer], past_ref[layer]], axis=1)
        mix_t = mix_ref[layer].T
        reach = segment + min(MARGIN, DMAX * (layer + 1))
        ahead[layer, 0 : 2 * channels, reach : reach + DMAX] = jnp.zeros((2 * channels, DMAX), BF16)
        for start, stop in reversed(chunks_of(0, reach)):
            size = stop - start
            if layer == layer_count - 1:
                grad_b = cot[:, start:stop]
                grad = grad_b.astype(F32)
            else:
                grad = dfield[:, start:stop]
                grad_b = grad.astype(BF16)
            filt = gates[layer, 0:channels, start:stop]
            sig = gates[layer, channels:, start:stop]
            dgate = jnp.dot(mix_t, grad_b, preferred_element_type=F32)
            dgate_sig = dgate * sig
            dpre = jnp.concatenate(
                [dgate_sig * (1.0 - filt * filt), dgate_sig * filt * (1.0 - sig)], axis=0
            ).astype(BF16)
            ahead[layer, 0 : 2 * channels, start:stop] = dpre
            later = moved(ahead[layer, 0 : 2 * channels, start : stop + DMAX], matrix)
            if start < segment:
                ahead[layer, 2 * channels :, start:stop] = grad_b
            grad = grad + jnp.dot(
                weight_t, jnp.concatenate([dpre, later], axis=0), preferred_element_type=F32
            )
            dfield[:, start:stop] = grad
            if layer > 0 or start >= segment:
                continue
            part = jnp.dot(
                lift_t, grad, preferred_element_type=F32, precision=lax.Precision.HIGHEST
            )
            part = jnp.concatenate([part, jnp.zeros((1, size), F32)], axis=0)
            for i in range(size // small):
                dinput_ref[start // small + i] = part[:, small * i : small * (i + 1)]
            for i in range(size // small):
                leave(start // small + i)


def weight_sums(mix_ref, grads_ref, inputs, seen, dfield, ahead):
    layer_count, channels = mix_ref.shape[:2]
    segment = seen.shape[2] - MARGIN
    taps, mixes = [], []
    for layer in range(layer_count):
        total = jnp.zeros((3 * channels, 3 * channels), F32)
        for start, stop in chunks_of(0, segment):
            total += lax.dot_general(
                seen[layer, :, start:stop], ahead[layer, :, start:stop],
                (((1,), (1,)), ((), ())), preferred_element_type=F32,
            )
        taps.append(total[: 2 * channels, : 2 * channels])
        mixes.append(total[2 * channels :, 2 * channels :].T)
    lift_total = jnp.zeros((3, channels), F32)
    for start, stop in chunks_of(0, segment):
        lift_total += lax.dot_general(
            inputs[:, MARGIN + start : MARGIN + stop], dfield[:, start:stop],
            (((1,), (1,)), ((), ())), preferred_element_type=F32,
            precision=lax.Precision.HIGHEST,
        )
    lift_block = jnp.concatenate([lift_total, jnp.zeros((channels - 3, channels), F32)], axis=0)
    taps.append(
        jnp.concatenate(
            [
                jnp.concatenate([mixes[0], mixes[1]], axis=1),
                jnp.concatenate([mixes[2], lift_block], axis=1),
            ],
            axis=0,
        )
    )
    rows = jnp.concatenate(taps, axis=0)
    grads_ref[...] = rows.reshape(grads_ref.shape).astype(BF16)


def whole_kernel(
    rows_count, cols_count,
    dil_ref, white_ref, cot_ref, lift_ref, now_ref, past_ref, mix_ref, factor_ref,
    cos_a_ref, sin_a_ref, cos_b_ref, sin_b_ref, spread_ref, local_ref, fast_ref,
    fast_back_ref, local_back_ref, gather_ref, twiddle_ref,
    out_ref, sums_ref,
    inputs, cot, field, seen, gates, dfield, ahead, left_halo, right_halo, cot_halo, dinput, grads,
    got_x, spectra, got_spectra, parts, got_parts, result, got_result,
    got_cols, part_sums, got_rows, own_sum, sums_rows, sums_all,
    send_sems, recv_sems,
):
    groups = rows_count * cols_count
    segment = white_ref.shape[1]
    small = segment // groups
    my_row, my_col = lax.axis_index("rows"), lax.axis_index("cols")
    me = my_row * cols_count + my_col
    cols = [my_col] + [lax.rem(my_col + j, cols_count) for j in range(1, cols_count)]
    rows = [my_row] + [lax.rem(my_row + i, rows_count) for i in range(1, rows_count)]

    def for_others(body):
        for col in cols[1:]:
            body(my_row, col)

        def one_row(step, carry):
            row = lax.rem(my_row + step, rows_count)
            for col in cols:
                body(row, col)
            return carry

        lax.fori_loop(1, rows_count, one_row, 0)

    def send(slot, source, target, row, col):
        pltpu.make_async_remote_copy(
            src_ref=source,
            dst_ref=target,
            send_sem=send_sems.at[slot],
            recv_sem=recv_sems.at[slot],
            device_id=(row, col),
            device_id_type=pl.DeviceIdType.MESH,
        ).start()

    def wait_for(sems, slot, landed):
        pltpu.make_async_copy(landed, landed, sems.at[slot]).wait()

    def exchange(slot, source, target):
        def one(row, col):
            send(slot, source.at[row * cols_count + col], target.at[me], row, col)

        for_others(one)
        target[me] = source[me]

    barrier = pltpu.get_barrier_semaphore()

    def greet(row, col):
        pl.semaphore_signal(
            barrier, inc=1, device_id=(row, col), device_id_type=pl.DeviceIdType.MESH
        )

    for_others(greet)

    after = lax.rem(me + 1, groups)
    ahead_of = lax.rem(me + groups - 1, groups)
    halo_slots = ((6, left_halo), (7, right_halo), (8, cot_halo))

    def before_halos():
        pl.semaphore_wait(barrier, groups - 1)
        row, col = after // cols_count, lax.rem(after, cols_count)
        send(6, white_ref.at[:, pl.ds(segment - MARGIN, MARGIN)], left_halo, row, col)
        row, col = ahead_of // cols_count, lax.rem(ahead_of, cols_count)
        send(7, white_ref.at[:, pl.ds(0, MARGIN)], right_halo, row, col)
        send(8, cot_ref.at[:, pl.ds(0, MARGIN)], cot_halo, row, col)

    def halos():
        for slot, landed in halo_slots:
            wait_for(recv_sems, slot, landed)
        left = jnp.where(me == 0, 0.0, left_halo[...])
        right = jnp.where(me == groups - 1, 0.0, right_halo[...])
        cot_right = jnp.where(me == groups - 1, 0.0, cot_halo[...].astype(F32)).astype(BF16)
        return left, right, cot_right

    def leave(block):
        @pl.when(me != block)
        def _():
            row, col = block // cols_count, block % cols_count
            send(0, dinput.at[block], got_x.at[me], row, col)

    layers(
        before_halos, halos, leave,
        dil_ref, white_ref, cot_ref, lift_ref, now_ref, past_ref, mix_ref,
        dinput, grads, inputs, cot, field, seen, gates, dfield, ahead,
    )

    flat = (4 * groups, small)
    cube = (groups, 4, small)

    def turned_by(values, cos_ref, sin_ref):
        here, turned = values
        cosine = jnp.broadcast_to(cos_ref[...][:, None, :], cube).reshape(flat)
        sine = jnp.broadcast_to(sin_ref[...][:, None, :], cube).reshape(flat)
        return (here * cosine + turned * sine).reshape(cube)

    got_x[me] = dinput[me]
    weight_sums(mix_ref, grads, inputs, seen, dfield, ahead)
    for col in cols[1:]:
        send(1, grads.at[:, col], got_cols.at[my_col], my_row, col)
    got_cols[my_col] = grads[:, my_col]

    wait_for(recv_sems, 0, got_x.at[pl.ds(0, groups - 1)])
    both = dot_left(spread_ref, got_x[...].reshape(flat))
    spectra[...] = turned_by((both[: 4 * groups], both[4 * groups :]), cos_a_ref, sin_a_ref)
    exchange(2, spectra, got_spectra)

    wait_for(recv_sems, 1, got_cols.at[pl.ds(0, cols_count - 1)])
    total = got_cols[0].astype(F32)
    for i in range(1, cols_count):
        total += got_cols[i].astype(F32)
    part_sums[...] = total
    for row in rows[1:]:
        send(3, part_sums.at[row], got_rows.at[my_row], row, my_col)
    got_rows[my_row] = part_sums[my_row]

    wait_for(recv_sems, 2, got_spectra.at[pl.ds(0, groups - 1)])
    both = dot_left(local_ref, got_spectra[...].reshape(flat))
    here, turned = both[: 4 * groups], both[4 * groups :]
    cosine, sine = twiddle_ref[0], twiddle_ref[1]
    pair = jnp.concatenate([here * cosine - turned * sine, turned * cosine + here * sine], axis=1)
    pair = dot_right(pair, fast_ref)
    factor = factor_ref[...]
    pair = jnp.concatenate([pair[:, :small] * factor, pair[:, small:] * factor], axis=1)
    pair = dot_right(pair, fast_back_ref)
    here, turned = pair[:, :small], pair[:, small:]
    pair = jnp.concatenate([here * cosine + turned * sine, turned * cosine - here * sine], axis=1)
    pair = dot_left(local_back_ref, pair)
    parts[...] = turned_by((pair[:, :small], pair[:, small:]), cos_b_ref, sin_b_ref)
    exchange(4, parts, got_parts)

    wait_for(recv_sems, 3, got_rows.at[pl.ds(0, rows_count - 1)])
    total = got_rows[0]
    for i in range(1, rows_count):
        total += got_rows[i]
    own_sum[...] = total.astype(BF16)
    for row in rows[1:]:
        send(9, own_sum, sums_rows.at[my_row], row, my_col)
    sums_rows[my_row] = own_sum[...]

    wait_for(recv_sems, 4, got_parts.at[pl.ds(0, groups - 1)])
    result[...] = dot_left(gather_ref, got_parts[...].reshape(flat)).reshape(cube)
    exchange(5, result, got_result)

    wait_for(recv_sems, 9, sums_rows.at[pl.ds(0, rows_count - 1)])
    for col in cols[1:]:
        send(10, sums_rows, sums_all.at[:, my_col], my_row, col)
    sums_all[:, my_col] = sums_rows[...]

    wait_for(recv_sems, 5, got_result.at[pl.ds(0, groups - 1)])
    out_ref[...] = got_result[...]
    wait_for(recv_sems, 10, sums_all.at[:, pl.ds(0, cols_count - 1)])
    sums_ref[...] = sums_all[...]

    for slot, sent in ((0, dinput), (2, spectra), (4, parts), (5, result)):
        wait_for(send_sems, slot, sent.at[pl.ds(0, groups - 1)])
    wait_for(send_sems, 1, got_cols.at[pl.ds(0, cols_count - 1)])
    wait_for(send_sems, 3, got_rows.at[pl.ds(0, rows_count - 1)])
    wait_for(send_sems, 9, sums_rows.at[pl.ds(0, rows_count - 1)])
    wait_for(send_sems, 10, sums_all.at[:, pl.ds(0, cols_count - 1)])
    for slot, landed in halo_slots:
        wait_for(send_sems, slot, landed)


def finish_kernel(scaling, out_ref, sums_ref, data_ref, now_ref, past_ref, mix_ref, lift_ref):
    layer_count, channels = mix_ref.shape[:2]
    if data_ref.ndim == 2:
        small = out_ref.shape[2]
        for i in range(out_ref.shape[0]):
            data_ref[:, small * i : small * (i + 1)] = out_ref[i][:3]
    else:
        data_ref[...] = out_ref[...]
    sums = sums_ref[...].astype(F32) * scaling
    for layer in range(layer_count):
        first = 2 * channels * layer
        now_ref[layer] = sums[first : first + channels]
        past_ref[layer] = sums[first + channels : first + 2 * channels]
    first = 2 * channels * layer_count
    mix_ref[0] = sums[first : first + channels, :channels]
    mix_ref[1] = sums[first : first + channels, channels:]
    mix_ref[2] = sums[first + channels :, :channels]
    lift_ref[...] = sums[first + channels : first + channels + 3, channels:]


def constants(rows_count, cols_count, small):
    groups = rows_count * cols_count
    segment = groups * small
    ids = np.arange(groups)
    residues = ids // cols_count + rows_count * (ids % cols_count)
    unit = np.eye(4)
    swap = np.kron(np.eye(2), np.array([[0.0, -1.0], [1.0, 0.0]]))
    take = np.diag([1.0, 1.0, 1.0, 0.0])

    def blocks(left, right, sign, inner):
        angle = sign * 2.0 * np.pi / groups * (np.outer(left, right) % groups)
        return np.kron(np.cos(angle), unit @ inner) + np.kron(np.sin(angle), swap @ inner)

    turn_all = np.kron(np.eye(groups), swap)
    spread = blocks(residues, ids, -1.0, take)
    local = blocks(ids, ids, -1.0, unit)
    local_back = blocks(ids, ids, 1.0, unit)
    gather = np.kron(np.eye(groups), take) @ blocks(ids, residues, 1.0, unit)
    gather = gather / float(segment * groups)
    lanes = np.arange(small)
    angle = 2.0 * np.pi / small * (np.outer(lanes, lanes) % small)
    cosine, sine = np.cos(angle), np.sin(angle)
    fast = np.block([[cosine, sine], [-sine, cosine]])
    fast_back = np.block([[cosine, -sine], [sine, cosine]])
    angle = 2.0 * np.pi / segment * (np.outer(ids, lanes) % segment)
    angle = np.repeat(angle, 4, axis=0)
    twiddle = np.stack([np.cos(angle), np.sin(angle)]).astype(np.float32)
    return (
        residues,
        halves(np.concatenate([spread, turn_all @ spread])),
        halves(np.concatenate([local, turn_all @ local])),
        halves(fast),
        halves(fast_back),
        halves(local_back),
        halves(gather),
        twiddle,
    )


def vmem():
    return pl.BlockSpec(memory_space=pltpu.VMEM)


def solution(mesh):
    rows_count, cols_count = mesh.shape["rows"], mesh.shape["cols"]
    groups = rows_count * cols_count

    def local(whitened, cotangent, lift, now, past, mix, dilations, psd_bin, psd_weight):
        segment = whitened.shape[1]
        layer_count, channels = mix.shape[:2]
        small = segment // groups
        length = segment * groups
        _, spread, local_m, fast, fast_back, local_back, gather, twiddle = constants(
            rows_count, cols_count, small
        )
        wide = small == TILE
        bins = psd_bin.reshape(small, groups).T.reshape(-1, TILE)
        factor, cos_a, sin_a, cos_b, sin_b, delays = pl.pallas_call(
            lambda *refs: prepare_kernel(rows_count, cols_count, length, *refs),
            out_shape=(jax.ShapeDtypeStruct((4 * bins.shape[0], TILE), F32),)
            + (jax.ShapeDtypeStruct((groups, small), F32),) * 4
            + (jax.ShapeDtypeStruct((layer_count, WIDE), jnp.int32),),
            in_specs=[pl.BlockSpec(memory_space=pltpu.SMEM)] + [vmem()] * 2,
            out_specs=(vmem(),) * 6,
            name="prepare",
        )(dilations, bins, psd_weight)
        if not wide:
            factor = factor.reshape(-1, 4, TILE).transpose(1, 0, 2).reshape(4, groups, small)
            factor = factor.transpose(1, 0, 2).reshape(4 * groups, small)

        grad_rows = 2 * channels * (layer_count + 1)
        reach = segment + MARGIN
        cube = (groups, 4, small)
        share = (grad_rows // groups, 2 * channels)
        shares = (rows_count, cols_count) + share
        out, sums = pl.pallas_call(
            lambda *refs: whole_kernel(rows_count, cols_count, *refs),
            out_shape=(
                jax.ShapeDtypeStruct(cube, F32),
                jax.ShapeDtypeStruct(shares, BF16),
            ),
            in_specs=[vmem()] * 19,
            out_specs=(vmem(),) * 2,
            scratch_shapes=[
                pltpu.VMEM((3, reach + MARGIN), F32),
                pltpu.VMEM((channels, reach), BF16),
                pltpu.VMEM((2, channels, FRONT + MARGIN + reach), F32),
                pltpu.VMEM((layer_count, 3 * channels, reach), BF16),
                pltpu.VMEM((layer_count, 2 * channels, reach), F32),
                pltpu.VMEM((channels, reach), F32),
                pltpu.VMEM((layer_count, 3 * channels, reach + DMAX), BF16),
                pltpu.VMEM((3, MARGIN), F32),
                pltpu.VMEM((3, MARGIN), F32),
                pltpu.VMEM((channels, MARGIN), BF16),
                pltpu.VMEM(cube, F32),
                pltpu.VMEM(shares, BF16),
            ]
            + [pltpu.VMEM(cube, F32)] * 7
            + [
                pltpu.VMEM((cols_count, rows_count) + share, BF16),
                pltpu.VMEM((rows_count,) + share, F32),
                pltpu.VMEM((rows_count,) + share, F32),
                pltpu.VMEM(share, BF16),
                pltpu.VMEM((rows_count,) + share, BF16),
                pltpu.VMEM(shares, BF16),
                pltpu.SemaphoreType.DMA((11,)),
                pltpu.SemaphoreType.DMA((11,)),
            ],
            compiler_params=pltpu.CompilerParams(
                collective_id=0, has_side_effects=True, vmem_limit_bytes=60 * 2**20
            ),
            name="whole",
        )(
            delays, whitened, cotangent, lift.T, now.transpose(0, 2, 1),
            past.transpose(0, 2, 1), mix, factor, cos_a, sin_a, cos_b, sin_b, spread, local_m,
            fast, fast_back, local_back, gather, twiddle,
        )
        scaling = 1.0 / math.sqrt(float(length))
        data, now_t, past_t, mixes, lift_t = pl.pallas_call(
            lambda *refs: finish_kernel(scaling, *refs),
            out_shape=(
                jax.ShapeDtypeStruct((3, segment) if wide else cube, F32),
                jax.ShapeDtypeStruct((layer_count, channels, 2 * channels), F32),
                jax.ShapeDtypeStruct((layer_count, channels, 2 * channels), F32),
                jax.ShapeDtypeStruct((layer_count, channels, channels), F32),
                jax.ShapeDtypeStruct((3, channels), F32),
            ),
            in_specs=[vmem()] * 2,
            out_specs=(vmem(),) * 5,
            name="finish",
        )(out, sums.reshape(grad_rows, 2 * channels))
        if not wide:
            data = data.transpose(1, 0, 2).reshape(4, segment)[:3]
        return data, now_t.transpose(0, 2, 1), past_t.transpose(0, 2, 1), mixes, lift_t.T

    in_specs = (
        P(None, ("rows", "cols")),
        P(None, ("rows", "cols")),
        P(),
        P(),
        P(),
        P(),
        P(),
        P(None, "cols", "rows"),
        P(),
    )
    out_specs = (P(None, ("rows", "cols")), P(), P(), P(), P())
    return jax.shard_map(local, mesh=mesh, in_specs=in_specs, out_specs=out_specs, check_vma=False)
```

```python
import math

import jax
import jax.numpy as jnp
import numpy as np
from jax import lax
from jax.experimental import pallas as pl
from jax.experimental.pallas import tpu as pltpu
from jax.sharding import PartitionSpec as P

DMAX = 256
TILE = 128
WIDE = 256
MARGIN = 640
FRONT = 384
F32 = jnp.float32
BF16 = jnp.bfloat16


def halves(matrix):
    high = matrix.astype(np.float32).astype(jnp.bfloat16)
    low = (matrix - high.astype(np.float64)).astype(np.float32).astype(jnp.bfloat16)
    return np.stack([high, low])


def split(values):
    high = values.astype(BF16)
    return high, (values - high.astype(F32)).astype(BF16)


def dot_left(pair_ref, values):
    high, low = split(values)
    total = jnp.dot(pair_ref[0], high, preferred_element_type=F32)
    total += jnp.dot(pair_ref[0], low, preferred_element_type=F32)
    return total + jnp.dot(pair_ref[1], high, preferred_element_type=F32)


def dot_right(values, pair_ref):
    high, low = split(values)
    total = jnp.dot(high, pair_ref[0], preferred_element_type=F32)
    total += jnp.dot(low, pair_ref[0], preferred_element_type=F32)
    return total + jnp.dot(high, pair_ref[1], preferred_element_type=F32)


def chunks_of(first, last, size=1024):
    cuts = sorted({first, last} | {x for x in range(0, last, size) if first < x < last})
    return list(zip(cuts[:-1], cuts[1:]))


def turns(angle_steps, length, sign):
    angle = sign * 2.0 * math.pi / length * lax.rem(angle_steps, length).astype(F32)
    return jnp.cos(angle), jnp.sin(angle)


def prepare_kernel(
    rows_count, cols_count, length,
    dil_ref, bins_ref, psd_ref,
    factor_ref, cos_a_ref, sin_a_ref, cos_b_ref, sin_b_ref, delays_ref,
):
    if bins_ref.ndim == 3:
        rows = bins_ref.shape[2] // TILE
        bins = jnp.concatenate(
            [bins_ref[0, :, TILE * i : TILE * (i + 1)] for i in range(rows)], axis=0
        )
    else:
        bins = bins_ref[...]
    entry_row = lax.shift_right_logical(bins, 7)
    entry_lane = jnp.bitwise_and(bins, TILE - 1)
    factors = []
    for kind in range(2):
        factor = jnp.zeros(bins.shape, F32)
        for row in range(psd_ref.shape[1] // TILE):
            table = psd_ref[kind : kind + 1, TILE * row : TILE * (row + 1)]
            table = jnp.broadcast_to(table, bins.shape)
            found = jnp.take_along_axis(table, entry_lane, axis=1)
            factor = jnp.where(entry_row == row, found, factor)
        if bins_ref.ndim == 3:
            turned = factor.T
            factor = jnp.concatenate(
                [turned[i : i + rows] for i in range(0, TILE, rows)], axis=1
            )
        factors.append(factor)
    signal = lax.broadcasted_iota(jnp.int32, (bins.shape[0], 4, TILE), 1)
    factor_ref[...] = jnp.where(
        signal < 2, factors[0][:, None, :], factors[1][:, None, :]
    ).reshape(factor_ref.shape)

    shape = cos_a_ref.shape
    groups, small = shape
    my_row, my_col = lax.axis_index("rows"), lax.axis_index("cols")
    me = my_row * cols_count + my_col
    residue = my_row + rows_count * my_col
    samples = lax.broadcasted_iota(jnp.int32, shape, 1)
    ids = lax.broadcasted_iota(jnp.int32, shape, 0)
    rows = sum((ids >= cols_count * i).astype(jnp.int32) for i in range(1, rows_count))
    residues = rows + rows_count * (ids - cols_count * rows)
    cos_a_ref[...], sin_a_ref[...] = turns(residues * (me * small + samples), length, -1.0)
    cos_b_ref[...], sin_b_ref[...] = turns(residue * (ids * small + samples), length, 1.0)
    for layer in range(dil_ref.shape[0]):
        delays_ref[layer : layer + 1, :] = jnp.full((1, WIDE), dil_ref[layer], jnp.int32)


def layers(
    before_halos, halos, leave,
    dil_ref, white_ref, cot_ref, lift_ref, now_ref, past_ref, mix_ref,
    dinput_ref, grads_ref, inputs, cot, field, seen, gates, dfield, ahead,
):
    segment = white_ref.shape[1]
    layer_count = mix_ref.shape[0]
    channels = mix_ref.shape[1]
    offset = lax.broadcasted_iota(jnp.int32, (DMAX + WIDE, WIDE), 0)
    offset -= lax.broadcasted_iota(jnp.int32, (DMAX + WIDE, WIDE), 1)

    def picks(distance):
        return jnp.where(offset == distance, 1.0, 0.0).astype(BF16)

    def moved(window, matrix):
        size = window.shape[1] - DMAX
        rows = window.shape[0]
        full = size // WIDE * WIDE
        pieces = []
        if full:
            stacked = jnp.concatenate(
                [window[:, i : i + DMAX + WIDE] for i in range(0, full, WIDE)], axis=0
            )
            found = jnp.dot(stacked, matrix, preferred_element_type=F32).astype(BF16)
            pieces = [found[rows * i : rows * (i + 1)] for i in range(full // WIDE)]
        if full < size:
            part = matrix[: DMAX + size - full, : size - full]
            found = jnp.dot(window[:, full:], part, preferred_element_type=F32)
            pieces.append(found.astype(BF16))
        return jnp.concatenate(pieces, axis=1)

    def at(column):
        return MARGIN + column

    inputs[:, MARGIN : MARGIN + segment] = white_ref[...]
    cot[:, 0:segment] = cot_ref[...]
    lift_t = lift_ref[...]
    lift = lift_t.T
    field[0, :, 0:FRONT] = jnp.zeros((channels, FRONT), F32)
    field[1, :, 0:FRONT] = jnp.zeros((channels, FRONT), F32)
    def lifted(start, stop):
        x = inputs[:, at(start) : at(stop)]
        field[0, :, FRONT + at(start) : FRONT + at(stop)] = (
            lift[:, 0:1] * x[0:1] + lift[:, 1:2] * x[1:2] + lift[:, 2:3] * x[2:3]
        )

    def in_order(layer, first):
        chunks = chunks_of(first, segment + MARGIN)
        if layer > 0:
            yield from chunks
            return
        inner = [c for c in chunks if DMAX <= c[0] and c[1] <= segment]
        yield from inner
        left, right, cot_right = halos()
        inputs[:, 0:MARGIN] = left
        inputs[:, MARGIN + segment :] = right
        cot[:, segment:] = cot_right
        lifted(-MARGIN, 0)
        lifted(segment, segment + MARGIN)
        yield from [c for c in chunks if c not in inner]

    for start, stop in chunks_of(0, segment):
        lifted(start, stop)
    before_halos()

    for layer in range(layer_count):
        delays = dil_ref[layer : layer + 1, :]
        matrix = picks(DMAX - delays)
        weight = jnp.concatenate([now_ref[layer], past_ref[layer]], axis=0).T
        mix = mix_ref[layer]
        source, target = layer % 2, (layer + 1) % 2
        first = -DMAX * (layer_count - 1 - layer)
        for start, stop in in_order(layer, first):
            size = stop - start
            place = FRONT + at(start)
            now = field[source, :, place : place + size]
            past = moved(field[source, :, place - DMAX : place + size].astype(BF16), matrix)
            both = jnp.concatenate([now.astype(BF16), past], axis=0)
            pre = jnp.dot(weight, both, preferred_element_type=F32)
            filt = jnp.tanh(pre[:channels])
            sig = 0.5 * jnp.tanh(0.5 * pre[channels:]) + 0.5
            gate = (filt * sig).astype(BF16)
            if layer + 1 < layer_count:
                field[target, :, place : place + size] = now + jnp.dot(
                    mix, gate, preferred_element_type=F32
                )
            if start >= 0:
                seen[layer, 0 : 2 * channels, start:stop] = both
                seen[layer, 2 * channels :, start:stop] = gate
                gates[layer, 0:channels, start:stop] = filt
                gates[layer, channels:, start:stop] = sig

    small = dinput_ref.shape[2]
    for layer in reversed(range(layer_count)):
        delays = dil_ref[layer : layer + 1, :]
        matrix = picks(delays)
        weight_t = jnp.concatenate([now_ref[layer], past_ref[layer]], axis=1)
        mix_t = mix_ref[layer].T
        reach = segment + min(MARGIN, DMAX * (layer + 1))
        ahead[layer, 0 : 2 * channels, reach : reach + DMAX] = jnp.zeros((2 * channels, DMAX), BF16)
        for start, stop in reversed(chunks_of(0, reach)):
            size = stop - start
            if layer == layer_count - 1:
                grad_b = cot[:, start:stop]
                grad = grad_b.astype(F32)
            else:
                grad = dfield[:, start:stop]
                grad_b = grad.astype(BF16)
            filt = gates[layer, 0:channels, start:stop]
            sig = gates[layer, channels:, start:stop]
            dgate = jnp.dot(mix_t, grad_b, preferred_element_type=F32)
            dgate_sig = dgate * sig
            dpre = jnp.concatenate(
                [dgate_sig * (1.0 - filt * filt), dgate_sig * filt * (1.0 - sig)], axis=0
            ).astype(BF16)
            ahead[layer, 0 : 2 * channels, start:stop] = dpre
            later = moved(ahead[layer, 0 : 2 * channels, start : stop + DMAX], matrix)
            if start < segment:
                ahead[layer, 2 * channels :, start:stop] = grad_b
            grad = grad + jnp.dot(
                weight_t, jnp.concatenate([dpre, later], axis=0), preferred_element_type=F32
            )
            dfield[:, start:stop] = grad
            if layer > 0 or start >= segment:
                continue
            part = jnp.dot(
                lift_t, grad, preferred_element_type=F32, precision=lax.Precision.HIGHEST
            )
            part = jnp.concatenate([part, jnp.zeros((1, size), F32)], axis=0)
            for i in range(size // small):
                dinput_ref[start // small + i] = part[:, small * i : small * (i + 1)]
            for i in range(size // small):
                leave(start // small + i)


def weight_sums(mix_ref, grads_ref, inputs, seen, dfield, ahead):
    layer_count, channels = mix_ref.shape[:2]
    segment = seen.shape[2] - MARGIN
    taps, mixes = [], []
    for layer in range(layer_count):
        total = jnp.zeros((3 * channels, 3 * channels), F32)
        for start, stop in chunks_of(0, segment):
            total += lax.dot_general(
                seen[layer, :, start:stop], ahead[layer, :, start:stop],
                (((1,), (1,)), ((), ())), preferred_element_type=F32,
            )
        taps.append(total[: 2 * channels, : 2 * channels])
        mixes.append(total[2 * channels :, 2 * channels :].T)
    lift_total = jnp.zeros((3, channels), F32)
    for start, stop in chunks_of(0, segment):
        lift_total += lax.dot_general(
            inputs[:, MARGIN + start : MARGIN + stop], dfield[:, start:stop],
            (((1,), (1,)), ((), ())), preferred_element_type=F32,
            precision=lax.Precision.HIGHEST,
        )
    lift_block = jnp.concatenate([lift_total, jnp.zeros((channels - 3, channels), F32)], axis=0)
    taps.append(
        jnp.concatenate(
            [
                jnp.concatenate([mixes[0], mixes[1]], axis=1),
                jnp.concatenate([mixes[2], lift_block], axis=1),
            ],
            axis=0,
        )
    )
    rows = jnp.concatenate(taps, axis=0)
    grads_ref[...] = rows.reshape(grads_ref.shape).astype(BF16)


def whole_kernel(
    rows_count, cols_count,
    dil_ref, white_ref, cot_ref, lift_ref, now_ref, past_ref, mix_ref, factor_ref,
    cos_a_ref, sin_a_ref, cos_b_ref, sin_b_ref, spread_ref, local_ref, fast_ref,
    fast_back_ref, local_back_ref, gather_ref, twiddle_ref,
    out_ref, sums_ref,
    inputs, cot, field, seen, gates, dfield, ahead, left_halo, right_halo, cot_halo, dinput, grads,
    got_x, spectra, got_spectra, parts, got_parts, result, got_result,
    got_cols, part_sums, got_rows, own_sum, sums_rows, sums_all,
    send_sems, recv_sems,
):
    groups = rows_count * cols_count
    segment = white_ref.shape[1]
    small = segment // groups
    my_row, my_col = lax.axis_index("rows"), lax.axis_index("cols")
    me = my_row * cols_count + my_col
    cols = [my_col] + [lax.rem(my_col + j, cols_count) for j in range(1, cols_count)]
    rows = [my_row] + [lax.rem(my_row + i, rows_count) for i in range(1, rows_count)]

    def for_others(body):
        for col in cols[1:]:
            body(my_row, col)

        def one_row(step, carry):
            row = lax.rem(my_row + step, rows_count)
            for col in cols:
                body(row, col)
            return carry

        lax.fori_loop(1, rows_count, one_row, 0)

    def send(slot, source, target, row, col):
        pltpu.make_async_remote_copy(
            src_ref=source,
            dst_ref=target,
            send_sem=send_sems.at[slot],
            recv_sem=recv_sems.at[slot],
            device_id=(row, col),
            device_id_type=pl.DeviceIdType.MESH,
        ).start()

    def wait_for(sems, slot, landed):
        pltpu.make_async_copy(landed, landed, sems.at[slot]).wait()

    def exchange(slot, source, target):
        def one(row, col):
            send(slot, source.at[row * cols_count + col], target.at[me], row, col)

        for_others(one)
        target[me] = source[me]

    barrier = pltpu.get_barrier_semaphore()

    def greet(row, col):
        pl.semaphore_signal(
            barrier, inc=1, device_id=(row, col), device_id_type=pl.DeviceIdType.MESH
        )

    for_others(greet)

    after = lax.rem(me + 1, groups)
    ahead_of = lax.rem(me + groups - 1, groups)
    halo_slots = ((6, left_halo), (7, right_halo), (8, cot_halo))

    def before_halos():
        pl.semaphore_wait(barrier, groups - 1)
        row, col = after // cols_count, lax.rem(after, cols_count)
        send(6, white_ref.at[:, pl.ds(segment - MARGIN, MARGIN)], left_halo, row, col)
        row, col = ahead_of // cols_count, lax.rem(ahead_of, cols_count)
        send(7, white_ref.at[:, pl.ds(0, MARGIN)], right_halo, row, col)
        send(8, cot_ref.at[:, pl.ds(0, MARGIN)], cot_halo, row, col)

    def halos():
        for slot, landed in halo_slots:
            wait_for(recv_sems, slot, landed)
        left = jnp.where(me == 0, 0.0, left_halo[...])
        right = jnp.where(me == groups - 1, 0.0, right_halo[...])
        cot_right = jnp.where(me == groups - 1, 0.0, cot_halo[...].astype(F32)).astype(BF16)
        return left, right, cot_right

    def leave(block):
        @pl.when(me != block)
        def _():
            row, col = block // cols_count, block % cols_count
            send(0, dinput.at[block], got_x.at[me], row, col)

    layers(
        before_halos, halos, leave,
        dil_ref, white_ref, cot_ref, lift_ref, now_ref, past_ref, mix_ref,
        dinput, grads, inputs, cot, field, seen, gates, dfield, ahead,
    )

    flat = (4 * groups, small)
    cube = (groups, 4, small)

    def turned_by(values, cos_ref, sin_ref):
        here, turned = values
        cosine = jnp.broadcast_to(cos_ref[...][:, None, :], cube).reshape(flat)
        sine = jnp.broadcast_to(sin_ref[...][:, None, :], cube).reshape(flat)
        return (here * cosine + turned * sine).reshape(cube)

    got_x[me] = dinput[me]
    weight_sums(mix_ref, grads, inputs, seen, dfield, ahead)
    for col in cols[1:]:
        send(1, grads.at[:, col], got_cols.at[my_col], my_row, col)
    got_cols[my_col] = grads[:, my_col]

    wait_for(recv_sems, 0, got_x.at[pl.ds(0, groups - 1)])
    both = dot_left(spread_ref, got_x[...].reshape(flat))
    spectra[...] = turned_by((both[: 4 * groups], both[4 * groups :]), cos_a_ref, sin_a_ref)
    exchange(2, spectra, got_spectra)

    wait_for(recv_sems, 1, got_cols.at[pl.ds(0, cols_count - 1)])
    total = got_cols[0].astype(F32)
    for i in range(1, cols_count):
        total += got_cols[i].astype(F32)
    part_sums[...] = total
    for row in rows[1:]:
        send(3, part_sums.at[row], got_rows.at[my_row], row, my_col)
    got_rows[my_row] = part_sums[my_row]

    wait_for(recv_sems, 2, got_spectra.at[pl.ds(0, groups - 1)])

    wait_for(recv_sems, 3, got_rows.at[pl.ds(0, rows_count - 1)])
    total = got_rows[0]
    for i in range(1, rows_count):
        total += got_rows[i]
    own_sum[...] = total.astype(BF16)
    for row in rows[1:]:
        send(9, own_sum, sums_rows.at[my_row], row, my_col)
    sums_rows[my_row] = own_sum[...]

    both = dot_left(local_ref, got_spectra[...].reshape(flat))
    here, turned = both[: 4 * groups], both[4 * groups :]
    cosine, sine = twiddle_ref[0], twiddle_ref[1]
    pair = jnp.concatenate([here * cosine - turned * sine, turned * cosine + here * sine], axis=1)
    pair = dot_right(pair, fast_ref)
    factor = factor_ref[...]
    pair = jnp.concatenate([pair[:, :small] * factor, pair[:, small:] * factor], axis=1)
    pair = dot_right(pair, fast_back_ref)
    here, turned = pair[:, :small], pair[:, small:]
    pair = jnp.concatenate([here * cosine + turned * sine, turned * cosine - here * sine], axis=1)
    pair = dot_left(local_back_ref, pair)
    parts[...] = turned_by((pair[:, :small], pair[:, small:]), cos_b_ref, sin_b_ref)
    exchange(4, parts, got_parts)

    wait_for(recv_sems, 9, sums_rows.at[pl.ds(0, rows_count - 1)])
    for col in cols[1:]:
        send(10, sums_rows, sums_all.at[:, my_col], my_row, col)
    sums_all[:, my_col] = sums_rows[...]

    wait_for(recv_sems, 4, got_parts.at[pl.ds(0, groups - 1)])
    result[...] = dot_left(gather_ref, got_parts[...].reshape(flat)).reshape(cube)
    exchange(5, result, got_result)

    wait_for(recv_sems, 5, got_result.at[pl.ds(0, groups - 1)])
    out_ref[...] = got_result[...]
    wait_for(recv_sems, 10, sums_all.at[:, pl.ds(0, cols_count - 1)])
    sums_ref[...] = sums_all[...]

    for slot, sent in ((0, dinput), (2, spectra), (4, parts), (5, result)):
        wait_for(send_sems, slot, sent.at[pl.ds(0, groups - 1)])
    wait_for(send_sems, 1, got_cols.at[pl.ds(0, cols_count - 1)])
    wait_for(send_sems, 3, got_rows.at[pl.ds(0, rows_count - 1)])
    wait_for(send_sems, 9, sums_rows.at[pl.ds(0, rows_count - 1)])
    wait_for(send_sems, 10, sums_all.at[:, pl.ds(0, cols_count - 1)])
    for slot, landed in halo_slots:
        wait_for(send_sems, slot, landed)


def finish_kernel(scaling, out_ref, sums_ref, data_ref, now_ref, past_ref, mix_ref, lift_ref):
    layer_count, channels = mix_ref.shape[:2]
    if data_ref.ndim == 2:
        small = out_ref.shape[2]
        for i in range(out_ref.shape[0]):
            data_ref[:, small * i : small * (i + 1)] = out_ref[i][:3]
    else:
        data_ref[...] = out_ref[...]
    sums = sums_ref[...].astype(F32) * scaling
    for layer in range(layer_count):
        first = 2 * channels * layer
        now_ref[layer] = sums[first : first + channels]
        past_ref[layer] = sums[first + channels : first + 2 * channels]
    first = 2 * channels * layer_count
    mix_ref[0] = sums[first : first + channels, :channels]
    mix_ref[1] = sums[first : first + channels, channels:]
    mix_ref[2] = sums[first + channels :, :channels]
    lift_ref[...] = sums[first + channels : first + channels + 3, channels:]


def constants(rows_count, cols_count, small):
    groups = rows_count * cols_count
    segment = groups * small
    ids = np.arange(groups)
    residues = ids // cols_count + rows_count * (ids % cols_count)
    unit = np.eye(4)
    swap = np.kron(np.eye(2), np.array([[0.0, -1.0], [1.0, 0.0]]))
    take = np.diag([1.0, 1.0, 1.0, 0.0])

    def blocks(left, right, sign, inner):
        angle = sign * 2.0 * np.pi / groups * (np.outer(left, right) % groups)
        return np.kron(np.cos(angle), unit @ inner) + np.kron(np.sin(angle), swap @ inner)

    turn_all = np.kron(np.eye(groups), swap)
    spread = blocks(residues, ids, -1.0, take)
    local = blocks(ids, ids, -1.0, unit)
    local_back = blocks(ids, ids, 1.0, unit)
    gather = np.kron(np.eye(groups), take) @ blocks(ids, residues, 1.0, unit)
    gather = gather / float(segment * groups)
    lanes = np.arange(small)
    order = lanes
    if small == TILE:
        order = lanes.reshape(groups, small // groups).T.reshape(-1)
    angle = 2.0 * np.pi / small * (np.outer(lanes, order) % small)
    cosine, sine = np.cos(angle), np.sin(angle)
    fast = np.block([[cosine, sine], [-sine, cosine]])
    fast_back = np.block([[cosine.T, -sine.T], [sine.T, cosine.T]])
    angle = 2.0 * np.pi / segment * (np.outer(ids, lanes) % segment)
    angle = np.repeat(angle, 4, axis=0)
    twiddle = np.stack([np.cos(angle), np.sin(angle)]).astype(np.float32)
    return (
        residues,
        halves(np.concatenate([spread, turn_all @ spread])),
        halves(np.concatenate([local, turn_all @ local])),
        halves(fast),
        halves(fast_back),
        halves(local_back),
        halves(gather),
        twiddle,
    )


def vmem():
    return pl.BlockSpec(memory_space=pltpu.VMEM)


def solution(mesh):
    rows_count, cols_count = mesh.shape["rows"], mesh.shape["cols"]
    groups = rows_count * cols_count

    def local(whitened, cotangent, lift, now, past, mix, dilations, psd_bin, psd_weight):
        segment = whitened.shape[1]
        layer_count, channels = mix.shape[:2]
        small = segment // groups
        length = segment * groups
        _, spread, local_m, fast, fast_back, local_back, gather, twiddle = constants(
            rows_count, cols_count, small
        )
        wide = small == TILE
        if wide:
            bins = psd_bin.transpose(1, 2, 0)
        else:
            bins = psd_bin.reshape(small, groups).T.reshape(-1, TILE)
        factor, cos_a, sin_a, cos_b, sin_b, delays = pl.pallas_call(
            lambda *refs: prepare_kernel(rows_count, cols_count, length, *refs),
            out_shape=(jax.ShapeDtypeStruct((4 * (segment // TILE), TILE), F32),)
            + (jax.ShapeDtypeStruct((groups, small), F32),) * 4
            + (jax.ShapeDtypeStruct((layer_count, WIDE), jnp.int32),),
            in_specs=[pl.BlockSpec(memory_space=pltpu.SMEM)] + [vmem()] * 2,
            out_specs=(vmem(),) * 6,
            name="prepare",
        )(dilations, bins, psd_weight)
        if not wide:
            factor = factor.reshape(-1, 4, TILE).transpose(1, 0, 2).reshape(4, groups, small)
            factor = factor.transpose(1, 0, 2).reshape(4 * groups, small)

        grad_rows = 2 * channels * (layer_count + 1)
        reach = segment + MARGIN
        cube = (groups, 4, small)
        share = (grad_rows // groups, 2 * channels)
        shares = (rows_count, cols_count) + share
        out, sums = pl.pallas_call(
            lambda *refs: whole_kernel(rows_count, cols_count, *refs),
            out_shape=(
                jax.ShapeDtypeStruct(cube, F32),
                jax.ShapeDtypeStruct(shares, BF16),
            ),
            in_specs=[vmem()] * 19,
            out_specs=(vmem(),) * 2,
            scratch_shapes=[
                pltpu.VMEM((3, reach + MARGIN), F32),
                pltpu.VMEM((channels, reach), BF16),
                pltpu.VMEM((2, channels, FRONT + MARGIN + reach), F32),
                pltpu.VMEM((layer_count, 3 * channels, reach), BF16),
                pltpu.VMEM((layer_count, 2 * channels, reach), F32),
                pltpu.VMEM((channels, reach), F32),
                pltpu.VMEM((layer_count, 3 * channels, reach + DMAX), BF16),
                pltpu.VMEM((3, MARGIN), F32),
                pltpu.VMEM((3, MARGIN), F32),
                pltpu.VMEM((channels, MARGIN), BF16),
                pltpu.VMEM(cube, F32),
                pltpu.VMEM(shares, BF16),
            ]
            + [pltpu.VMEM(cube, F32)] * 7
            + [
                pltpu.VMEM((cols_count, rows_count) + share, BF16),
                pltpu.VMEM((rows_count,) + share, F32),
                pltpu.VMEM((rows_count,) + share, F32),
                pltpu.VMEM(share, BF16),
                pltpu.VMEM((rows_count,) + share, BF16),
                pltpu.VMEM(shares, BF16),
                pltpu.SemaphoreType.DMA((11,)),
                pltpu.SemaphoreType.DMA((11,)),
            ],
            compiler_params=pltpu.CompilerParams(
                collective_id=0, has_side_effects=True, vmem_limit_bytes=60 * 2**20
            ),
            name="whole",
        )(
            delays, whitened, cotangent, lift.T, now.transpose(0, 2, 1),
            past.transpose(0, 2, 1), mix, factor, cos_a, sin_a, cos_b, sin_b, spread, local_m,
            fast, fast_back, local_back, gather, twiddle,
        )
        scaling = 1.0 / math.sqrt(float(length))
        data, now_t, past_t, mixes, lift_t = pl.pallas_call(
            lambda *refs: finish_kernel(scaling, *refs),
            out_shape=(
                jax.ShapeDtypeStruct((3, segment) if wide else cube, F32),
                jax.ShapeDtypeStruct((layer_count, channels, 2 * channels), F32),
                jax.ShapeDtypeStruct((layer_count, channels, 2 * channels), F32),
                jax.ShapeDtypeStruct((layer_count, channels, channels), F32),
                jax.ShapeDtypeStruct((3, channels), F32),
            ),
            in_specs=[vmem()] * 2,
            out_specs=(vmem(),) * 5,
            name="finish",
        )(out, sums.reshape(grad_rows, 2 * channels))
        if not wide:
            data = data.transpose(1, 0, 2).reshape(4, segment)[:3]
        return data, now_t.transpose(0, 2, 1), past_t.transpose(0, 2, 1), mixes, lift_t.T

    in_specs = (
        P(None, ("rows", "cols")),
        P(None, ("rows", "cols")),
        P(),
        P(),
        P(),
        P(),
        P(),
        P(None, "cols", "rows"),
        P(),
    )
    out_specs = (P(None, ("rows", "cols")), P(), P(), P(), P())
    return jax.shard_map(local, mesh=mesh, in_specs=in_specs, out_specs=out_specs, check_vma=False)
```
